32 devices in a mesh: line: 4 (over x, core), shot: 8 (over z, y).
Axes of the slice: x: 2, y: 2, z: 4, core: 2. Of those that a mesh axis runs over, the one named last changes fastest.
Arguments:
- velocity: float32 [64, 128, 128], P('line', 'shot'), may hold values from 1.5 to 4.5
- density: float32 [64, 128, 128], P('line', 'shot'), may hold values from 1 to 3
- start_pressure: float32 [128, 256, 128], P('line', 'shot'), may hold values from -6 to 6
- observed: float32 [128, 256, 128], P('line', 'shot'), may hold values from -6 to 6
- corners: int32 [4, 8, 2], P('line', 'shot'), may hold values from 0 to 96, as said below
Outputs:
- grad_velocity: float32 [64, 128, 128], P('line', 'shot')
- grad_density: float32 [64, 128, 128], P('line', 'shot')
The draws below stay inside these ranges and needn't reach their ends.
Inputs may be any that keep to these rules, and one draw needn't show every extreme that they name: corners[a, b, 0] = min(max(a * 16 - 16 + r, 0), 32) and corners[a, b, 1] = min(max(b * 16 - 16 + t, 0), 96) for whole numbers r and t of 0 to 16.
All inputs are finite; a program needn't handle non-finite values.
Results may differ from the reference program's by a relative error of at most 0.0003.
Values sent between devices are 32-bit elements; how exact they have to be, the bound alone decides.
A program may use at most 64 MiB of HBM per device.

```python
import math
import jax
import jax.numpy as jnp
from jax import lax

BLOCK = 16
NZ = 128
APER = 32
GX = 64
GY = 128
N_LINE = 4
N_SHOT = 8


def draw_corners(key, part):
    offsets = jax.random.randint(key, (N_LINE, N_SHOT, 2), 0, BLOCK + 1)
    line_ids = jnp.arange(N_LINE, dtype=jnp.int32)[:, None]
    shot_ids = jnp.arange(N_SHOT, dtype=jnp.int32)[None, :]
    first = jnp.clip(line_ids * BLOCK - BLOCK + offsets[:, :, 0], 0, GX - 2 * BLOCK)
    second = jnp.clip(shot_ids * BLOCK - BLOCK + offsets[:, :, 1], 0, GY - 2 * BLOCK)
    return jnp.stack([first, second], axis=-1).astype(jnp.int32)


def levels(stream_key, extent, shards, least, largest):
    factor_of, own = 1.0, jax.random.fold_in(stream_key, 6)
    for axis_at, parts in shards:
        draws = jnp.exp(jax.random.uniform(jax.random.fold_in(own, axis_at), (parts,), jnp.float32, least / len(shards), largest / len(shards)))
        factor_of = factor_of * jnp.repeat(draws, extent[axis_at] // parts).reshape([-1 if axis == axis_at else 1 for axis in range(len(extent))])
    return factor_of


def noise(key, shape, scale, bound, cuts=(), held_as=jnp.bfloat16):
    array = scale * jax.random.normal(key, shape, jnp.float32)
    if cuts:
        array = array * levels(key, shape, cuts, -0.22, 0.18)
    return jnp.clip(array, -bound, bound).astype(held_as)


def setup_inputs(seed: int = 0) -> dict:
    keys = jax.random.split(jax.random.key(seed), 6)
    return {
        "velocity": jnp.clip(1.5 + 3.0 * jax.random.uniform(keys[0], (GX, GY, NZ), jnp.float32) ** levels(keys[0], (GX, GY, NZ), ((0, 4), (1, 8)), -0.2, 0.2), 1.5, 4.5),
        "density": jnp.clip(jnp.exp(math.log(3.0) - 1.0986123 * jax.random.uniform(keys[1], (GX, GY, NZ), jnp.float32) ** levels(keys[1], (GX, GY, NZ), ((0, 4), (1, 8)), -0.2, 0.2)), 1.0, 3.0),
        "start_pressure": noise(keys[2], (N_LINE * APER, N_SHOT * APER, NZ), 1.0, 6.0, ((0, 4), (1, 8)), jnp.float32),
        "observed": noise(keys[3], (N_LINE * APER, N_SHOT * APER, NZ), 1.0, 6.0, ((0, 4), (1, 8)), jnp.float32),
        "corners": draw_corners(jax.random.fold_in(keys[5], 71), 0),
    }


coeffs = (1225.0 / 1024.0, -245.0 / 3072.0, 49.0 / 5120.0, -5.0 / 7168.0)
time_ratio = 0.1
wavelet = (20.0, -12.0)

def deriv_plus(field, axis):
    widths = [(0, 0)] * 3
    widths[axis] = (4, 4)
    padded = jnp.pad(field, widths)
    count = field.shape[axis]
    total = jnp.zeros_like(field)
    for m in range(1, 5):
        upper = lax.slice_in_dim(padded, 4 + m, 4 + m + count, axis=axis)
        lower = lax.slice_in_dim(padded, 5 - m, 5 - m + count, axis=axis)
        total = total + coeffs[m - 1] * (upper - lower)
    return total

def deriv_minus(field, axis):
    widths = [(0, 0)] * 3
    widths[axis] = (4, 4)
    padded = jnp.pad(field, widths)
    count = field.shape[axis]
    total = jnp.zeros_like(field)
    for m in range(1, 5):
        upper = lax.slice_in_dim(padded, 3 + m, 3 + m + count, axis=axis)
        lower = lax.slice_in_dim(padded, 4 - m, 4 - m + count, axis=axis)
        total = total + coeffs[m - 1] * (upper - lower)
    return total

def shot_misfit(model, pressure, observed):
    speed = model[0]
    dense = model[1]
    vel_x = jnp.zeros_like(pressure)
    vel_y = jnp.zeros_like(pressure)
    vel_z = jnp.zeros_like(pressure)
    centre = (pressure.shape[0] // 2, pressure.shape[1] // 2, pressure.shape[2] // 2)
    for level in range(2):
        vel_x = vel_x - time_ratio * deriv_plus(pressure, 0) / dense
        vel_y = vel_y - time_ratio * deriv_plus(pressure, 1) / dense
        vel_z = vel_z - time_ratio * deriv_plus(pressure, 2) / dense
        spread = deriv_minus(vel_x, 0) + deriv_minus(vel_y, 1) + deriv_minus(vel_z, 2)
        pressure = pressure - time_ratio * dense * speed * speed * spread
        pressure = pressure.at[centre].add(wavelet[level])
    misfit_term = pressure - observed
    return 0.5 * jnp.sum(misfit_term * misfit_term)

def reference(velocity, density, start_pressure, observed, corners):
    lines = corners.shape[0]
    shots = corners.shape[1]
    depth = velocity.shape[2]
    width = start_pressure.shape[0] // lines
    model = jnp.stack([velocity, density])
    zero_int = jnp.zeros((), jnp.int32)

    def visit(grads, index):
        line_index = (index // shots).astype(jnp.int32)
        shot_index = (index % shots).astype(jnp.int32)
        corner = corners[line_index, shot_index].astype(jnp.int32)
        place = (zero_int, corner[0], corner[1], zero_int)
        aperture = lax.dynamic_slice(model, place, (2, width, width, depth))
        spot = (line_index * width, shot_index * width, zero_int)
        pressure = lax.dynamic_slice(start_pressure, spot, (width, width, depth))
        seen = lax.dynamic_slice(observed, spot, (width, width, depth))
        local = jax.grad(shot_misfit)(aperture, pressure, seen)
        current = lax.dynamic_slice(grads, place, (2, width, width, depth))
        grads = lax.dynamic_update_slice(grads, current + local, place)
        return (grads, None)
    grads, unused = lax.scan(visit, jnp.zeros_like(model), jnp.arange(lines * shots, dtype=jnp.int32))
    return (grads[0], grads[1])
```

```python
import functools

import jax
import jax.numpy as jnp
import ml_dtypes
import numpy as np
from jax import lax
from jax.experimental import pallas as pl
from jax.experimental.pallas import tpu as pltpu
from jax.sharding import PartitionSpec as P

MESH = pl.DeviceIdType.MESH
coeffs = (1225.0 / 1024.0, -245.0 / 3072.0, 49.0 / 5120.0, -5.0 / 7168.0)
time_ratio = 0.1
wavelet = (20.0, -12.0)
RB = 4


def split(value):
    high = float(np.float32(value).astype(ml_dtypes.bfloat16))
    low = float(np.float32(value - high).astype(ml_dtypes.bfloat16))
    return high, low


def band(depth, plus):
    row = lax.broadcasted_iota(jnp.int32, (depth, depth), 0)
    col = lax.broadcasted_iota(jnp.int32, (depth, depth), 1)
    gap = row - col
    high = jnp.zeros((depth, depth), jnp.float32)
    low = jnp.zeros((depth, depth), jnp.float32)
    for m in range(1, 5):
        hi, lo = split(coeffs[m - 1])
        up, down = (m, 1 - m) if plus else (m - 1, -m)
        high = jnp.where(gap == up, hi, jnp.where(gap == down, -hi, high))
        low = jnp.where(gap == up, lo, jnp.where(gap == down, -lo, low))
    top = jnp.concatenate([high, low], axis=1)
    bottom = jnp.concatenate([high, jnp.zeros_like(low)], axis=1)
    return jnp.concatenate([top, bottom], axis=0).astype(jnp.bfloat16)


def along_z(rows, matrix):
    depth = rows[0].shape[1]
    width = rows[0].shape[0]
    field = jnp.concatenate(rows, axis=0)
    high = field.astype(jnp.bfloat16)
    low = (field - high.astype(jnp.float32)).astype(jnp.bfloat16)
    both = jnp.concatenate([high, low], axis=1)
    out = jnp.dot(both, matrix, preferred_element_type=jnp.float32)
    out = out[:, :depth] + out[:, depth:]
    return [out[k * width:(k + 1) * width] for k in range(len(rows))]


def combine(pairs):
    total = None
    for c, (upper, lower) in zip(coeffs, pairs):
        term = c * (upper - lower)
        total = term if total is None else total + term
    return total


def kernel(
    n_line, n_shot,
    corner, vel_in, rho_in, p_in, obs_in,
    vel_out, rho_out,
    ext_v, ext_r, grad_v, grad_r,
    p0, p1, a2, a1, vx1, vx2, bx, vy1, vy2, by,
    ex, ey, ez, zd, inv, kk, s1, ss, q2, vz1, vz2, rr, obs, w_plus, w_minus,
    sl, rl, zs, zr, ys, yr,
    fy_s, fy_r, fz_s, fz_r, fl_s, fl_r, rl_s, rl_r, rz_s, rz_r, ry_s, ry_r,
):
    block, _, depth = vel_in.shape
    width = p_in.shape[0]
    a = lax.axis_index("line")
    b = lax.axis_index("shot")
    odd = lax.rem(b, 2)
    partner = b + 1 - 2 * odd
    onward = b + 2 - 4 * odd
    behind = b - 2 + 4 * odd
    has_onward = (onward >= 0) & (onward < n_shot)
    has_behind = (behind >= 0) & (behind < n_shot)
    line_to = (a - 1, a + 1)
    has_line = (a > 0, a < n_line - 1)
    near = 2 * (1 - odd)
    far = 2 * odd
    exts = (ext_v, ext_r)
    ins = (vel_in, rho_in)
    outs = (vel_out, rho_out)
    grads = (grad_v, grad_r)

    barrier = pltpu.get_barrier_semaphore()

    def greet(there):
        pl.semaphore_signal(barrier, inc=1, device_id=there, device_id_type=MESH)

    greet((a, partner))
    pl.when(has_onward)(lambda: greet((a, onward)))
    pl.when(has_behind)(lambda: greet((a, behind)))
    pl.when(has_line[0])(lambda: greet((a - 1, b)))
    pl.when(has_line[1])(lambda: greet((a + 1, b)))
    one = jnp.int32(1)
    none = jnp.int32(0)
    count = one
    for there in (has_onward, has_behind, has_line[0], has_line[1]):
        count = count + jnp.where(there, one, none)
    pl.semaphore_wait(barrier, count)

    def cols(slot):
        return pl.ds(pl.multiple_of(slot * block, block), block)

    mid = pl.ds(block, block)

    def remote(src, dst, send, recv, there):
        return pltpu.make_async_remote_copy(
            src_ref=src, dst_ref=dst, send_sem=send, recv_sem=recv,
            device_id=there, device_id_type=MESH,
        )

    def fwd_y(k):
        return remote(ins[k], exts[k].at[mid, cols(far), :], fy_s.at[k], fy_r.at[k], (a, partner))

    def fwd_z(k):
        return remote(
            exts[k].at[mid, cols(near), :], exts[k].at[mid, cols(far), :],
            fz_s.at[k], fz_r.at[k], (a, onward),
        )

    def fwd_line(k, piece, side):
        slot = (1, near, far)[piece]
        src = ins[k] if piece == 0 else exts[k].at[mid, cols(slot), :]
        dst = exts[k].at[pl.ds(2 * block * (1 - side), block), cols(slot), :]
        return remote(
            src, dst, fl_s.at[k, piece, side], fl_r.at[k, piece, side], (line_to[side], b)
        )

    def start_line(k, piece):
        for side in range(2):
            pl.when(has_line[side])(lambda side=side: fwd_line(k, piece, side).start())

    for k in (1, 0):
        fwd_y(k).start()
        start_line(k, 0)

    for k in range(2):
        exts[k][block:2 * block, block:2 * block, :] = ins[k][...]
    for field in (p0, p1, a2, a1):
        field[0:4, :, :] = jnp.zeros((4, width + 16, depth), jnp.float32)
        field[width + 4:width + 8, :, :] = jnp.zeros((4, width + 16, depth), jnp.float32)
    for field in (vx1, vx2, bx):
        field[0:4, :, :] = jnp.zeros((4, width, depth), jnp.float32)
        field[width + 4:width + 8, :, :] = jnp.zeros((4, width, depth), jnp.float32)

    def clear(i, carry):
        nothing = jnp.zeros((8, depth), jnp.float32)
        for field, at in ((p0, 4), (p1, 4), (a2, 4), (a1, 4), (vy1, 0), (vy2, 0), (by, 0)):
            field[i + at, 0:8, :] = nothing
            field[i + at, width + 8:width + 16, :] = nothing
        p0[i + 4, 8:width + 8, :] = p_in[i]
        obs[i] = obs_in[i]
        return carry

    lax.fori_loop(0, width, clear, 0)
    w_plus[...] = band(depth, True)
    w_minus[...] = band(depth, False)
    wide = 2 * block + width
    for grad in grads:
        def clear_grad(i, carry, grad=grad):
            grad[i] = jnp.zeros((wide, depth), jnp.float32)
            return carry
        lax.fori_loop(0, wide, clear_grad, 0)

    steps = width // RB

    def over(step):
        def body(i, carry):
            step([i * RB + k for k in range(RB)])
            return carry
        lax.fori_loop(0, steps, body, 0)

    def dx_plus(f, i):
        return combine([(f[i + 4 + m, 8:width + 8, :], f[i + 5 - m, 8:width + 8, :]) for m in range(1, 5)])

    def dy_plus(f, i):
        return combine([(f[i + 4, 8 + m:width + 8 + m, :], f[i + 4, 9 - m:width + 9 - m, :]) for m in range(1, 5)])

    def dx_minus(f, i):
        return combine([(f[i + 3 + m], f[i + 4 - m]) for m in range(1, 5)])

    def dy_minus(f, i):
        return combine([(f[i, 7 + m:width + 7 + m, :], f[i, 8 - m:width + 8 - m, :]) for m in range(1, 5)])

    def body_rows(f, i):
        return f[i + 4, 8:width + 8, :]

    def put_rows(f, i, value):
        f[i + 4, 8:width + 8, :] = value

    def stage_a(rows):
        z = along_z([p_in[i] for i in rows], w_plus[...])
        for i, dz in zip(rows, z):
            ex[i] = dx_plus(p0, i)
            ey[i] = dy_plus(p0, i)
            ez[i] = dz

    over(stage_a)
    lane = lax.broadcasted_iota(jnp.int32, (1, depth), 1)
    spot = jnp.where(lane == depth // 2, 1.0, 0.0).astype(jnp.float32)
    half = width // 2
    p0[half + 4, half + 8:half + 9, :] = p0[half + 4, half + 8:half + 9, :] + wavelet[0] * spot
    obs[half, half:half + 1, :] = obs[half, half:half + 1, :] - wavelet[1] * spot

    for k in (1, 0):
        fwd_y(k).wait_recv()
        pl.when(has_onward)(lambda: fwd_z(k).start())
        start_line(k, 1)
    for k in (1, 0):
        @pl.when(has_behind)
        def _():
            fwd_z(k).wait_recv()
            start_line(k, 2)

    def finish_halo(k):
        for piece in range(3):
            for side in range(2):
                there = has_line[side]
                if piece == 2:
                    there = there & has_behind
                pl.when(there)(lambda: fwd_line(k, piece, 1 - side).wait_recv())

    shift_x = jnp.minimum(jnp.maximum(corner[0] - (a - 1) * block, 0), block)
    shift_y = jnp.minimum(jnp.maximum(corner[1] - (b - 1) * block, 0), block)

    def aperture(ext, i):
        return ext[shift_x + i, pl.ds(shift_y, width), :]

    def stage_b(rows):
        vz = []
        for i in rows:
            r = 1.0 / aperture(ext_r, i)
            inv[i] = r
            t = -time_ratio * r
            vx1[i + 4] = t * ex[i]
            vy1[i, 8:width + 8, :] = t * ey[i]
            z = t * ez[i]
            vz1[i] = z
            vz.append(z)
        for i, d in zip(rows, along_z(vz, w_minus[...])):
            zd[i] = d

    def stage_c(rows):
        for i in rows:
            v = aperture(ext_v, i)
            k = time_ratio * aperture(ext_r, i) * v * v
            s = dx_minus(vx1, i) + dy_minus(vy1, i) + zd[i]
            kk[i] = k
            s1[i] = s
            put_rows(p1, i, body_rows(p0, i) - k * s)

    def stage_d(rows):
        vz = []
        z = along_z([body_rows(p1, i) for i in rows], w_plus[...])
        for i, dz in zip(rows, z):
            t = -time_ratio * inv[i]
            vx2[i + 4] = vx1[i + 4] + t * dx_plus(p1, i)
            vy2[i, 8:width + 8, :] = vy1[i, 8:width + 8, :] + t * dy_plus(p1, i)
            v = vz1[i] + t * dz
            vz2[i] = v
            vz.append(v)
        for i, d in zip(rows, along_z(vz, w_minus[...])):
            zd[i] = d

    def stage_e(rows):
        for i in rows:
            s = dx_minus(vx2, i) + dy_minus(vy2, i) + zd[i]
            k = kk[i]
            q = body_rows(p1, i) - k * s - obs[i]
            q2[i] = q
            ss[i] = s * q
            put_rows(a2, i, -k * q)

    def stage_f(rows):
        bz = []
        z = along_z([body_rows(a2, i) for i in rows], w_plus[...])
        for i, dz in zip(rows, z):
            r = inv[i]
            dx = dx_plus(a2, i)
            dy = dy_plus(a2, i)
            rr[i] = dx * vx2[i + 4] + dy * vy2[i, 8:width + 8, :] + dz * vz2[i]
            bx[i + 4] = r * dx
            by[i, 8:width + 8, :] = r * dy
            bz.append(r * dz)
        for i, d in zip(rows, along_z(bz, w_minus[...])):
            zd[i] = d

    def stage_g(rows):
        for i in rows:
            q1 = q2[i] - time_ratio * (dx_minus(bx, i) + dy_minus(by, i) + zd[i])
            put_rows(a1, i, -kk[i] * q1)
            s = ss[i] + s1[i] * q1
            ss[i] = s
            grad_v[i + block, block:block + width, :] = (
                -2.0 * time_ratio * aperture(ext_r, i) * aperture(ext_v, i) * s
            )

    def stage_h(rows):
        z = along_z([body_rows(a1, i) for i in rows], w_plus[...])
        for i, dz in zip(rows, z):
            total = rr[i] + dx_plus(a1, i) * vx1[i + 4]
            total = total + dy_plus(a1, i) * vy1[i, 8:width + 8, :] + dz * vz1[i]
            v = aperture(ext_v, i)
            grad_r[i + block, block:block + width, :] = inv[i] * total - time_ratio * v * v * ss[i]

    def back_line(k, slot, side):
        return remote(
            sl.at[k, slot, side], rl.at[k, slot, side], rl_s.at[k, slot, side], rl_r.at[k, slot, side],
            (line_to[side], b),
        )

    def back_z(k):
        return remote(zs.at[k], zr.at[k], rz_s.at[k], rz_r.at[k], (a, behind))

    def back_y(k):
        return remote(ys.at[k], yr.at[k], ry_s.at[k], ry_r.at[k], (a, partner))

    def term(k, slot_x, slot_y, i):
        return grads[k][block + slot_x * block - shift_x + i, pl.ds(block + slot_y * block - shift_y, block), :]

    order = (far, near, 1)

    def send_line(k):
        for slot in order:
            for side in range(2):
                @pl.when(has_line[side])
                def _():
                    def fill(i, carry):
                        sl[k, slot, side, i] = term(k, 2 * side, slot, i)
                        return carry
                    lax.fori_loop(0, block, fill, 0)
                    back_line(k, slot, side).start()

    for side in range(2):
        @pl.when(jnp.logical_not(has_line[side]))
        def _():
            for k in range(2):
                for slot in range(3):
                    rl[k, slot, 1 - side] = jnp.zeros((block, block, depth), jnp.float32)

    @pl.when(jnp.logical_not(has_onward))
    def _():
        for k in range(2):
            zr[k] = jnp.zeros((block, block, depth), jnp.float32)

    finish_halo(1)
    over(stage_b)
    finish_halo(0)
    over(stage_c)
    over(stage_d)
    over(stage_e)
    over(stage_f)
    over(stage_g)
    send_line(0)
    over(stage_h)
    send_line(1)

    def wait_line(k, slot):
        for side in range(2):
            pl.when(has_line[side])(lambda: back_line(k, slot, 1 - side).wait_recv())

    def gather(k, slot, out, extra):
        wait_line(k, slot)
        if extra is not None:
            extra[1]()
        def add(i, carry):
            total = term(k, 1, slot, i) + rl[k, slot, 0, i] + rl[k, slot, 1, i]
            if extra is not None:
                total = total + extra[0][k, i]
            out[i] = total
            return carry
        lax.fori_loop(0, block, add, 0)

    for k in range(2):
        @pl.when(has_behind)
        def _():
            gather(k, far, zs.at[k], None)
            back_z(k).start()
        @pl.when(jnp.logical_not(has_behind))
        def _():
            wait_line(k, far)
    for k in range(2):
        gather(k, near, ys.at[k], (zr, lambda: pl.when(has_onward)(lambda: back_z(k).wait_recv())))
        back_y(k).start()
    for k in range(2):
        gather(k, 1, outs[k], (yr, lambda: back_y(k).wait_recv()))

    for k in range(2):
        fwd_y(k).wait_send()
        back_y(k).wait_send()
        pl.when(has_onward)(lambda: fwd_z(k).wait_send())
        pl.when(has_behind)(lambda: back_z(k).wait_send())
        for side in range(2):
            @pl.when(has_line[side])
            def _():
                for piece in range(2):
                    fwd_line(k, piece, side).wait_send()
                for slot in order:
                    back_line(k, slot, side).wait_send()
            pl.when(has_line[side] & has_behind)(lambda: fwd_line(k, 2, side).wait_send())


def body(n_line, n_shot, velocity, density, start_pressure, observed, corners):
    block, _, depth = velocity.shape
    width = start_pressure.shape[0]
    cells = jax.ShapeDtypeStruct(velocity.shape, jnp.float32)

    def scratch(*shape):
        return pltpu.VMEM(shape, jnp.float32)

    padded = scratch(width + 8, width + 16, depth)
    along_x = scratch(width + 8, width, depth)
    along_y = scratch(width, width + 16, depth)
    plain = scratch(width, width, depth)
    extended = scratch(3 * block, 3 * block, depth)
    wide = scratch(2 * block + width, 2 * block + width, depth)
    matrix = pltpu.VMEM((2 * depth, 2 * depth), jnp.bfloat16)
    pieces = scratch(2, 3, 2, block, block, depth)
    pair = scratch(2, block, block, depth)
    sem = pltpu.SemaphoreType.DMA
    vmem = pl.BlockSpec(memory_space=pltpu.VMEM)
    return pl.pallas_call(
        functools.partial(kernel, n_line, n_shot),
        out_shape=(cells, cells),
        in_specs=[pl.BlockSpec(memory_space=pltpu.SMEM)] + [vmem] * 4,
        out_specs=(vmem, vmem),
        scratch_shapes=[extended] * 2 + [wide] * 2 + [padded] * 4 + [along_x] * 3 + [along_y] * 3
        + [plain] * 13 + [matrix] * 2 + [pieces] * 2 + [pair] * 4
        + [sem((2,))] * 4 + [sem((2, 3, 2))] * 4 + [sem((2,))] * 4,
        compiler_params=pltpu.CompilerParams(
            collective_id=0, has_side_effects=True, vmem_limit_bytes=56 * 1024 * 1024
        ),
    )(corners.reshape(2), velocity, density, start_pressure, observed)


def solution(mesh):
    placed = P("line", "shot", None)
    return jax.shard_map(
        functools.partial(body, mesh.shape["line"], mesh.shape["shot"]),
        mesh=mesh,
        in_specs=(placed,) * 5,
        out_specs=(placed, placed),
        check_vma=False,
    )
```

```python
import functools

import jax
import jax.numpy as jnp
import ml_dtypes
import numpy as np
from jax import lax
from jax.experimental import pallas as pl
from jax.experimental.pallas import tpu as pltpu
from jax.sharding import PartitionSpec as P

MESH = pl.DeviceIdType.MESH
coeffs = (1225.0 / 1024.0, -245.0 / 3072.0, 49.0 / 5120.0, -5.0 / 7168.0)
time_ratio = 0.1
wavelet = (20.0, -12.0)
RB = 4
RB_Z = 16


def split(value):
    high = float(np.float32(value).astype(ml_dtypes.bfloat16))
    low = float(np.float32(value - high).astype(ml_dtypes.bfloat16))
    return high, low


def band(depth, plus):
    row = lax.broadcasted_iota(jnp.int32, (depth, depth), 0)
    col = lax.broadcasted_iota(jnp.int32, (depth, depth), 1)
    gap = row - col
    high = jnp.zeros((depth, depth), jnp.float32)
    low = jnp.zeros((depth, depth), jnp.float32)
    for m in range(1, 5):
        hi, lo = split(coeffs[m - 1])
        up, down = (m, 1 - m) if plus else (m - 1, -m)
        high = jnp.where(gap == up, hi, jnp.where(gap == down, -hi, high))
        low = jnp.where(gap == up, lo, jnp.where(gap == down, -lo, low))
    top = jnp.concatenate([high, low], axis=1)
    bottom = jnp.concatenate([high, jnp.zeros_like(low)], axis=1)
    return jnp.concatenate([top, bottom], axis=0).astype(jnp.bfloat16)


def along_z(rows, matrix):
    depth = rows[0].shape[1]
    width = rows[0].shape[0]
    field = jnp.concatenate(rows, axis=0)
    high = field.astype(jnp.bfloat16)
    low = (field - high.astype(jnp.float32)).astype(jnp.bfloat16)
    both = jnp.concatenate([high, low], axis=1)
    out = jnp.dot(both, matrix, preferred_element_type=jnp.float32)
    out = out[:, :depth] + out[:, depth:]
    return [out[k * width:(k + 1) * width] for k in range(len(rows))]


def combine(pairs):
    total = None
    for c, (upper, lower) in zip(coeffs, pairs):
        term = c * (upper - lower)
        total = term if total is None else total + term
    return total


def kernel(
    n_line, n_shot,
    corner, vel_in, rho_in, p_in, obs_in,
    out,
    ext_v, ext_r, grad_v, grad_r,
    p0, p1, a2, a1, vx1, vx2, bx, vy1, vy2, by,
    ex, ey, ez, zd, inv, kk, s1, ss, q2, vz1, vz2, rr, obs, w_plus, w_minus,
    sl, rl, zs, zr, ys, yr,
    fy_s, fy_r, fz_s, fz_r, fl_s, fl_r, rl_s, rl_r, rz_s, rz_r, ry_s, ry_r,
):
    block, _, depth = vel_in.shape
    width = p_in.shape[0]
    a = lax.axis_index("line")
    b = lax.axis_index("shot")
    odd = lax.rem(b, 2)
    partner = b + 1 - 2 * odd
    onward = b + 2 - 4 * odd
    behind = b - 2 + 4 * odd
    has_onward = (onward >= 0) & (onward < n_shot)
    has_behind = (behind >= 0) & (behind < n_shot)
    line_to = (a - 1, a + 1)
    has_line = (a > 0, a < n_line - 1)
    near = 2 * (1 - odd)
    far = 2 * odd
    exts = (ext_v, ext_r)
    ins = (vel_in, rho_in)
    grads = (grad_v, grad_r)

    barrier = pltpu.get_barrier_semaphore()

    def greet(there):
        pl.semaphore_signal(barrier, inc=1, device_id=there, device_id_type=MESH)

    greet((a, partner))
    pl.when(has_onward)(lambda: greet((a, onward)))
    pl.when(has_behind)(lambda: greet((a, behind)))
    pl.when(has_line[0])(lambda: greet((a - 1, b)))
    pl.when(has_line[1])(lambda: greet((a + 1, b)))
    one = jnp.int32(1)
    none = jnp.int32(0)
    count = one
    for there in (has_onward, has_behind, has_line[0], has_line[1]):
        count = count + jnp.where(there, one, none)
    pl.semaphore_wait(barrier, count)

    def cols(slot):
        return pl.ds(pl.multiple_of(slot * block, block), block)

    mid = pl.ds(block, block)

    def remote(src, dst, send, recv, there):
        return pltpu.make_async_remote_copy(
            src_ref=src, dst_ref=dst, send_sem=send, recv_sem=recv,
            device_id=there, device_id_type=MESH,
        )

    def fwd_y(k):
        return remote(ins[k], exts[k].at[mid, cols(far), :], fy_s.at[k], fy_r.at[k], (a, partner))

    def fwd_z(k):
        return remote(
            exts[k].at[mid, cols(near), :], exts[k].at[mid, cols(far), :],
            fz_s.at[k], fz_r.at[k], (a, onward),
        )

    def fwd_line(k, piece, side):
        slot = (1, near, far)[piece]
        src = ins[k] if piece == 0 else exts[k].at[mid, cols(slot), :]
        dst = exts[k].at[pl.ds(2 * block * (1 - side), block), cols(slot), :]
        return remote(
            src, dst, fl_s.at[k, piece, side], fl_r.at[k, piece, side], (line_to[side], b)
        )

    def start_line(k, piece):
        for side in range(2):
            pl.when(has_line[side])(lambda side=side: fwd_line(k, piece, side).start())

    for k in (1, 0):
        fwd_y(k).start()
        start_line(k, 0)

    for k in range(2):
        exts[k][block:2 * block, block:2 * block, :] = ins[k][...]
    for field in (p0, p1, a2, a1):
        field[0:4, :, :] = jnp.zeros((4, width + 16, depth), jnp.float32)
        field[width + 4:width + 8, :, :] = jnp.zeros((4, width + 16, depth), jnp.float32)
    for field in (vx1, vx2, bx):
        field[0:4, :, :] = jnp.zeros((4, width, depth), jnp.float32)
        field[width + 4:width + 8, :, :] = jnp.zeros((4, width, depth), jnp.float32)

    def clear(i, carry):
        nothing = jnp.zeros((8, depth), jnp.float32)
        for field, at in ((p0, 4), (p1, 4), (a2, 4), (a1, 4), (vy1, 0), (vy2, 0), (by, 0)):
            field[i + at, 0:8, :] = nothing
            field[i + at, width + 8:width + 16, :] = nothing
        p0[i + 4, 8:width + 8, :] = p_in[i]
        obs[i] = obs_in[i]
        return carry

    lax.fori_loop(0, width, clear, 0)
    w_plus[...] = band(depth, True)
    w_minus[...] = band(depth, False)
    wide = 2 * block + width
    for grad in grads:
        def clear_grad(i, carry, grad=grad):
            grad[i] = jnp.zeros((wide, depth), jnp.float32)
            return carry
        lax.fori_loop(0, wide, clear_grad, 0)

    def over(step, size=RB):
        def body(i, carry):
            step([i * size + k for k in range(size)])
            return carry
        lax.fori_loop(0, width // size, body, 0)

    def dx_plus(f, i):
        return combine([(f[i + 4 + m, 8:width + 8, :], f[i + 5 - m, 8:width + 8, :]) for m in range(1, 5)])

    def dy_plus(f, i):
        return combine([(f[i + 4, 8 + m:width + 8 + m, :], f[i + 4, 9 - m:width + 9 - m, :]) for m in range(1, 5)])

    def dx_minus(f, i):
        return combine([(f[i + 3 + m], f[i + 4 - m]) for m in range(1, 5)])

    def dy_minus(f, i):
        return combine([(f[i, 7 + m:width + 7 + m, :], f[i, 8 - m:width + 8 - m, :]) for m in range(1, 5)])

    def body_rows(f, i):
        return f[i + 4, 8:width + 8, :]

    def put_rows(f, i, value):
        f[i + 4, 8:width + 8, :] = value

    def stage_a(rows):
        z = along_z([p_in[i] for i in rows], w_plus[...])
        for i, dz in zip(rows, z):
            ex[i] = dx_plus(p0, i)
            ey[i] = dy_plus(p0, i)
            ez[i] = dz

    over(stage_a, RB_Z)
    lane = lax.broadcasted_iota(jnp.int32, (1, depth), 1)
    spot = jnp.where(lane == depth // 2, 1.0, 0.0).astype(jnp.float32)
    half = width // 2
    p0[half + 4, half + 8:half + 9, :] = p0[half + 4, half + 8:half + 9, :] + wavelet[0] * spot
    obs[half, half:half + 1, :] = obs[half, half:half + 1, :] - wavelet[1] * spot

    for k in (1, 0):
        fwd_y(k).wait_recv()
        pl.when(has_onward)(lambda: fwd_z(k).start())
        start_line(k, 1)
    for k in (1, 0):
        @pl.when(has_behind)
        def _():
            fwd_z(k).wait_recv()
            start_line(k, 2)

    def finish_halo(k):
        for piece in range(3):
            for side in range(2):
                there = has_line[side]
                if piece == 2:
                    there = there & has_behind
                pl.when(there)(lambda: fwd_line(k, piece, 1 - side).wait_recv())

    shift_x = jnp.minimum(jnp.maximum(corner[0] - (a - 1) * block, 0), block)
    shift_y = jnp.minimum(jnp.maximum(corner[1] - (b - 1) * block, 0), block)

    def aperture(ext, i):
        return ext[shift_x + i, pl.ds(shift_y, width), :]

    def stage_b(rows):
        vz = []
        for i in rows:
            r = 1.0 / aperture(ext_r, i)
            inv[i] = r
            t = -time_ratio * r
            vx1[i + 4] = t * ex[i]
            vy1[i, 8:width + 8, :] = t * ey[i]
            z = t * ez[i]
            vz1[i] = z
            vz.append(z)
        for i, d in zip(rows, along_z(vz, w_minus[...])):
            zd[i] = d

    def stage_c(rows):
        for i in rows:
            v = aperture(ext_v, i)
            k = time_ratio * aperture(ext_r, i) * v * v
            s = dx_minus(vx1, i) + dy_minus(vy1, i) + zd[i]
            kk[i] = k
            s1[i] = s
            put_rows(p1, i, body_rows(p0, i) - k * s)

    def stage_d(rows):
        vz = []
        z = along_z([body_rows(p1, i) for i in rows], w_plus[...])
        for i, dz in zip(rows, z):
            t = -time_ratio * inv[i]
            vx2[i + 4] = vx1[i + 4] + t * dx_plus(p1, i)
            vy2[i, 8:width + 8, :] = vy1[i, 8:width + 8, :] + t * dy_plus(p1, i)
            v = vz1[i] + t * dz
            vz2[i] = v
            vz.append(v)
        for i, d in zip(rows, along_z(vz, w_minus[...])):
            zd[i] = d

    def stage_e(rows):
        for i in rows:
            s = dx_minus(vx2, i) + dy_minus(vy2, i) + zd[i]
            k = kk[i]
            q = body_rows(p1, i) - k * s - obs[i]
            q2[i] = q
            ss[i] = s * q
            put_rows(a2, i, -k * q)

    def stage_f(rows):
        bz = []
        z = along_z([body_rows(a2, i) for i in rows], w_plus[...])
        for i, dz in zip(rows, z):
            r = inv[i]
            dx = dx_plus(a2, i)
            dy = dy_plus(a2, i)
            rr[i] = dx * vx2[i + 4] + dy * vy2[i, 8:width + 8, :] + dz * vz2[i]
            bx[i + 4] = r * dx
            by[i, 8:width + 8, :] = r * dy
            bz.append(r * dz)
        for i, d in zip(rows, along_z(bz, w_minus[...])):
            zd[i] = d

    def stage_g(rows):
        for i in rows:
            q1 = q2[i] - time_ratio * (dx_minus(bx, i) + dy_minus(by, i) + zd[i])
            put_rows(a1, i, -kk[i] * q1)
            s = ss[i] + s1[i] * q1
            ss[i] = s
            grad_v[i + block, block:block + width, :] = (
                -2.0 * time_ratio * aperture(ext_r, i) * aperture(ext_v, i) * s
            )

    def stage_h(rows):
        z = along_z([body_rows(a1, i) for i in rows], w_plus[...])
        for i, dz in zip(rows, z):
            total = rr[i] + dx_plus(a1, i) * vx1[i + 4]
            total = total + dy_plus(a1, i) * vy1[i, 8:width + 8, :] + dz * vz1[i]
            v = aperture(ext_v, i)
            grad_r[i + block, block:block + width, :] = inv[i] * total - time_ratio * v * v * ss[i]

    def back_line(k, slot, side):
        return remote(
            sl.at[k, slot, side], rl.at[k, slot, side], rl_s.at[k, slot, side], rl_r.at[k, slot, side],
            (line_to[side], b),
        )

    def back_z(k):
        return remote(zs.at[k], zr.at[k], rz_s.at[k], rz_r.at[k], (a, behind))

    def back_y(k):
        return remote(ys.at[k], yr.at[k], ry_s.at[k], ry_r.at[k], (a, partner))

    def term(k, slot_x, slot_y, i):
        return grads[k][block + slot_x * block - shift_x + i, pl.ds(block + slot_y * block - shift_y, block), :]

    order = (far, near, 1)

    def send_line(k):
        for slot in order:
            for side in range(2):
                @pl.when(has_line[side])
                def _():
                    def fill(i, carry):
                        sl[k, slot, side, i] = term(k, 2 * side, slot, i)
                        return carry
                    lax.fori_loop(0, block, fill, 0)
                    back_line(k, slot, side).start()

    for side in range(2):
        @pl.when(jnp.logical_not(has_line[side]))
        def _():
            for k in range(2):
                for slot in range(3):
                    rl[k, slot, 1 - side] = jnp.zeros((block, block, depth), jnp.float32)

    @pl.when(jnp.logical_not(has_onward))
    def _():
        for k in range(2):
            zr[k] = jnp.zeros((block, block, depth), jnp.float32)

    finish_halo(1)
    over(stage_b, RB_Z)
    finish_halo(0)
    over(stage_c)
    over(stage_d, RB_Z)
    over(stage_e)
    over(stage_f, RB_Z)
    over(stage_g)
    send_line(0)
    over(stage_h, RB_Z)
    send_line(1)

    def wait_line(k, slot):
        for side in range(2):
            pl.when(has_line[side])(lambda: back_line(k, slot, 1 - side).wait_recv())

    def gather(k, slot, out, extra):
        wait_line(k, slot)
        if extra is not None:
            extra[1]()
        def add(i, carry):
            total = term(k, 1, slot, i) + rl[k, slot, 0, i] + rl[k, slot, 1, i]
            if extra is not None:
                total = total + extra[0][k, i]
            out[i] = total
            return carry
        lax.fori_loop(0, block, add, 0)

    for k in range(2):
        @pl.when(has_behind)
        def _():
            gather(k, far, zs.at[k], None)
            back_z(k).start()
        @pl.when(jnp.logical_not(has_behind))
        def _():
            wait_line(k, far)
    for k in range(2):
        gather(k, near, ys.at[k], (zr, lambda: pl.when(has_onward)(lambda: back_z(k).wait_recv())))
        back_y(k).start()
    for k in range(2):
        gather(k, 1, out.at[k], (yr, lambda: back_y(k).wait_recv()))

    for k in range(2):
        fwd_y(k).wait_send()
        back_y(k).wait_send()
        pl.when(has_onward)(lambda: fwd_z(k).wait_send())
        pl.when(has_behind)(lambda: back_z(k).wait_send())
        for side in range(2):
            @pl.when(has_line[side])
            def _():
                for piece in range(2):
                    fwd_line(k, piece, side).wait_send()
                for slot in order:
                    back_line(k, slot, side).wait_send()
            pl.when(has_line[side] & has_behind)(lambda: fwd_line(k, 2, side).wait_send())


def apart(both, vel_out, rho_out):
    vel_out[...] = both[0]
    rho_out[...] = both[1]


def body(n_line, n_shot, velocity, density, start_pressure, observed, corners):
    block, _, depth = velocity.shape
    width = start_pressure.shape[0]
    cells = jax.ShapeDtypeStruct(velocity.shape, jnp.float32)

    def scratch(*shape):
        return pltpu.VMEM(shape, jnp.float32)

    padded = scratch(width + 8, width + 16, depth)
    along_x = scratch(width + 8, width, depth)
    along_y = scratch(width, width + 16, depth)
    plain = scratch(width, width, depth)
    extended = scratch(3 * block, 3 * block, depth)
    wide = scratch(2 * block + width, 2 * block + width, depth)
    matrix = pltpu.VMEM((2 * depth, 2 * depth), jnp.bfloat16)
    pieces = scratch(2, 3, 2, block, block, depth)
    pair = scratch(2, block, block, depth)
    sem = pltpu.SemaphoreType.DMA
    vmem = pl.BlockSpec(memory_space=pltpu.VMEM)
    both = pl.pallas_call(
        functools.partial(kernel, n_line, n_shot),
        out_shape=jax.ShapeDtypeStruct((2,) + velocity.shape, jnp.float32),
        in_specs=[pl.BlockSpec(memory_space=pltpu.SMEM)] + [vmem] * 4,
        out_specs=vmem,
        scratch_shapes=[extended] * 2 + [wide] * 2 + [padded] * 4 + [along_x] * 3 + [along_y] * 3
        + [plain] * 13 + [matrix] * 2 + [pieces] * 2 + [pair] * 4
        + [sem((2,))] * 4 + [sem((2, 3, 2))] * 4 + [sem((2,))] * 4,
        compiler_params=pltpu.CompilerParams(
            collective_id=0, has_side_effects=True, vmem_limit_bytes=56 * 1024 * 1024
        ),
    )(corners.reshape(2), velocity, density, start_pressure, observed)
    return pl.pallas_call(
        apart, out_shape=(cells, cells), in_specs=[vmem], out_specs=(vmem, vmem)
    )(both)


def solution(mesh):
    placed = P("line", "shot", None)
    return jax.shard_map(
        functools.partial(body, mesh.shape["line"], mesh.shape["shot"]),
        mesh=mesh,
        in_specs=(placed,) * 5,
        out_specs=(placed, placed),
        check_vma=False,
    )
```

```python
import functools

import jax
import jax.numpy as jnp
import ml_dtypes
import numpy as np
from jax import lax
from jax.experimental import pallas as pl
from jax.experimental.pallas import tpu as pltpu
from jax.sharding import PartitionSpec as P

MESH = pl.DeviceIdType.MESH
coeffs = (1225.0 / 1024.0, -245.0 / 3072.0, 49.0 / 5120.0, -5.0 / 7168.0)
time_ratio = 0.1
wavelet = (20.0, -12.0)
RB = 4
RB_Z = 16


def split(value):
    high = float(np.float32(value).astype(ml_dtypes.bfloat16))
    low = float(np.float32(value - high).astype(ml_dtypes.bfloat16))
    return high, low


def band(depth, plus):
    row = lax.broadcasted_iota(jnp.int32, (depth, depth), 0)
    col = lax.broadcasted_iota(jnp.int32, (depth, depth), 1)
    gap = row - col
    high = jnp.zeros((depth, depth), jnp.float32)
    low = jnp.zeros((depth, depth), jnp.float32)
    for m in range(1, 5):
        hi, lo = split(coeffs[m - 1])
        up, down = (m, 1 - m) if plus else (m - 1, -m)
        high = jnp.where(gap == up, hi, jnp.where(gap == down, -hi, high))
        low = jnp.where(gap == up, lo, jnp.where(gap == down, -lo, low))
    top = jnp.concatenate([high, low], axis=1)
    bottom = jnp.concatenate([high, jnp.zeros_like(low)], axis=1)
    return jnp.concatenate([top, bottom], axis=0).astype(jnp.bfloat16)


def along_z(rows, matrix):
    depth = rows[0].shape[1]
    width = rows[0].shape[0]
    field = jnp.concatenate(rows, axis=0)
    high = field.astype(jnp.bfloat16)
    low = (field - high.astype(jnp.float32)).astype(jnp.bfloat16)
    both = jnp.concatenate([high, low], axis=1)
    out = jnp.dot(both, matrix, preferred_element_type=jnp.float32)
    out = out[:, :depth] + out[:, depth:]
    return [out[k * width:(k + 1) * width] for k in range(len(rows))]


def combine(pairs):
    total = None
    for c, (upper, lower) in zip(coeffs, pairs):
        term = c * (upper - lower)
        total = term if total is None else total + term
    return total


def kernel(
    n_line, n_shot,
    corner, vel_in, rho_in, p_in, obs_in,
    out,
    ext_v, ext_r, grad_v, grad_r,
    p0, p1, a2, a1, vx1, vx2, bx, vy1, vy2, by,
    ex, ey, ez, zd, inv, kk, s1, ss, q2, vz1, vz2, rr, obs, dens, speed, w_plus, w_minus,
    sl, rl, zs, zr, ys, yr,
    fy_s, fy_r, fz_s, fz_r, fl_s, fl_r, rl_s, rl_r, rz_s, rz_r, ry_s, ry_r,
):
    block, _, depth = vel_in.shape
    width = p_in.shape[0]
    a = lax.axis_index("line")
    b = lax.axis_index("shot")
    odd = lax.rem(b, 2)
    partner = b + 1 - 2 * odd
    onward = b + 2 - 4 * odd
    behind = b - 2 + 4 * odd
    has_onward = (onward >= 0) & (onward < n_shot)
    has_behind = (behind >= 0) & (behind < n_shot)
    line_to = (a - 1, a + 1)
    has_line = (a > 0, a < n_line - 1)
    near = 2 * (1 - odd)
    far = 2 * odd
    exts = (ext_v, ext_r)
    ins = (vel_in, rho_in)
    grads = (grad_v, grad_r)

    barrier = pltpu.get_barrier_semaphore()

    def greet(there):
        pl.semaphore_signal(barrier, inc=1, device_id=there, device_id_type=MESH)

    greet((a, partner))
    pl.when(has_onward)(lambda: greet((a, onward)))
    pl.when(has_behind)(lambda: greet((a, behind)))
    pl.when(has_line[0])(lambda: greet((a - 1, b)))
    pl.when(has_line[1])(lambda: greet((a + 1, b)))
    one = jnp.int32(1)
    none = jnp.int32(0)
    count = one
    for there in (has_onward, has_behind, has_line[0], has_line[1]):
        count = count + jnp.where(there, one, none)
    pl.semaphore_wait(barrier, count)

    def cols(slot):
        return pl.ds(pl.multiple_of(slot * block, block), block)

    mid = pl.ds(block, block)

    def remote(src, dst, send, recv, there):
        return pltpu.make_async_remote_copy(
            src_ref=src, dst_ref=dst, send_sem=send, recv_sem=recv,
            device_id=there, device_id_type=MESH,
        )

    def fwd_y(k):
        return remote(ins[k], exts[k].at[mid, cols(far), :], fy_s.at[k], fy_r.at[k], (a, partner))

    def fwd_z(k):
        return remote(
            exts[k].at[mid, cols(near), :], exts[k].at[mid, cols(far), :],
            fz_s.at[k], fz_r.at[k], (a, onward),
        )

    def fwd_line(k, piece, side):
        slot = (1, near, far)[piece]
        src = ins[k] if piece == 0 else exts[k].at[mid, cols(slot), :]
        dst = exts[k].at[pl.ds(2 * block * (1 - side), block), cols(slot), :]
        return remote(
            src, dst, fl_s.at[k, piece, side], fl_r.at[k, piece, side], (line_to[side], b)
        )

    def start_line(k, piece):
        for side in range(2):
            pl.when(has_line[side])(lambda side=side: fwd_line(k, piece, side).start())

    for k in (1, 0):
        fwd_y(k).start()
        start_line(k, 0)

    for k in range(2):
        exts[k][block:2 * block, block:2 * block, :] = ins[k][...]
    for field in (p0, p1, a2, a1, vx1, vx2, bx):
        field[0:4, :, :] = jnp.zeros((4, width, depth), jnp.float32)
        field[width + 4:width + 8, :, :] = jnp.zeros((4, width, depth), jnp.float32)

    turns = width // 8

    def reorder(i, carry):
        for t in range(turns):
            p0[i + 4, 8 * t:8 * t + 8, :] = p_in[i, pl.ds(t, 8, turns), :]
            obs[i, 8 * t:8 * t + 8, :] = obs_in[i, pl.ds(t, 8, turns), :]
        return carry

    lax.fori_loop(0, width, reorder, 0)
    w_plus[...] = band(depth, True)
    w_minus[...] = band(depth, False)
    wide = 2 * block + width
    for grad in grads:
        def clear_grad(i, carry, grad=grad):
            grad[i] = jnp.zeros((wide, depth), jnp.float32)
            return carry
        lax.fori_loop(0, wide, clear_grad, 0)

    def over(step, size=RB):
        def body(i, carry):
            step([i * size + k for k in range(size)])
            return carry
        lax.fori_loop(0, width // size, body, 0)

    sub = lax.broadcasted_iota(jnp.int32, (8, depth), 0)

    def reach(row):
        f = [row[8 * t:8 * t + 8] for t in range(turns)]
        down = [jnp.where(sub == 0, 0.0, pltpu.roll(x, 1, 0)) for x in f]
        up = [jnp.where(sub == 7, 0.0, pltpu.roll(x, 7, 0)) for x in f]
        return down + f + up

    def dx_plus(f, i):
        return combine([(f[i + 4 + m], f[i + 5 - m]) for m in range(1, 5)])

    def dy_plus(f, i):
        near_by = reach(f[i + 4])
        parts = []
        for t in range(turns, 2 * turns):
            parts.append(combine([(near_by[t + m], near_by[t + 1 - m]) for m in range(1, 5)]))
        return jnp.concatenate(parts, axis=0)

    def dxy_minus(fx, fy, i):
        near_by = reach(fy[i])
        total = None
        for m in range(1, 5):
            gap = fx[i + 3 + m] - fx[i + 4 - m]
            side = [near_by[t + m - 1] - near_by[t - m] for t in range(turns, 2 * turns)]
            term = coeffs[m - 1] * (gap + jnp.concatenate(side, axis=0))
            total = term if total is None else total + term
        return total

    def stage_a(rows):
        z = along_z([p0[i + 4] for i in rows], w_plus[...])
        for i, dz in zip(rows, z):
            ex[i] = dx_plus(p0, i)
            ey[i] = dy_plus(p0, i)
            ez[i] = dz

    over(stage_a, RB_Z)
    lane = lax.broadcasted_iota(jnp.int32, (1, depth), 1)
    spot = jnp.where(lane == depth // 2, 1.0, 0.0).astype(jnp.float32)
    half = width // 2
    at = 8 * (half % turns) + half // turns
    p0[half + 4, at:at + 1, :] = p0[half + 4, at:at + 1, :] + wavelet[0] * spot
    obs[half, at:at + 1, :] = obs[half, at:at + 1, :] - wavelet[1] * spot

    for k in (1, 0):
        fwd_y(k).wait_recv()
        pl.when(has_onward)(lambda: fwd_z(k).start())
        start_line(k, 1)
    for k in (1, 0):
        @pl.when(has_behind)
        def _():
            fwd_z(k).wait_recv()
            start_line(k, 2)

    def finish_halo(k):
        for piece in range(3):
            for side in range(2):
                there = has_line[side]
                if piece == 2:
                    there = there & has_behind
                pl.when(there)(lambda: fwd_line(k, piece, 1 - side).wait_recv())

    shift_x = jnp.minimum(jnp.maximum(corner[0] - (a - 1) * block, 0), block)
    shift_y = jnp.minimum(jnp.maximum(corner[1] - (b - 1) * block, 0), block)

    def aperture(ext, i):
        parts = [ext[shift_x + i, pl.ds(shift_y + t, 8, turns), :] for t in range(turns)]
        return jnp.concatenate(parts, axis=0)

    def put_grad(grad, i, value):
        for t in range(turns):
            grad[i + block, pl.ds(block + t, 8, turns), :] = value[8 * t:8 * t + 8]

    def stage_b(rows):
        vz = []
        for i in rows:
            rho = aperture(ext_r, i)
            r = 1.0 / rho
            dens[i] = rho
            inv[i] = r
            t = -time_ratio * r
            vx1[i + 4] = t * ex[i]
            vy1[i] = t * ey[i]
            z = t * ez[i]
            vz1[i] = z
            vz.append(z)
        for i, d in zip(rows, along_z(vz, w_minus[...])):
            zd[i] = d

    def stage_c(rows):
        for i in rows:
            v = aperture(ext_v, i)
            k = time_ratio * dens[i] * v * v
            speed[i] = v
            s = dxy_minus(vx1, vy1, i) + zd[i]
            kk[i] = k
            s1[i] = s
            p1[i + 4] = p0[i + 4] - k * s

    def stage_d(rows):
        vz = []
        z = along_z([p1[i + 4] for i in rows], w_plus[...])
        for i, dz in zip(rows, z):
            t = -time_ratio * inv[i]
            vx2[i + 4] = vx1[i + 4] + t * dx_plus(p1, i)
            vy2[i] = vy1[i] + t * dy_plus(p1, i)
            v = vz1[i] + t * dz
            vz2[i] = v
            vz.append(v)
        for i, d in zip(rows, along_z(vz, w_minus[...])):
            zd[i] = d

    def stage_e(rows):
        for i in rows:
            s = dxy_minus(vx2, vy2, i) + zd[i]
            k = kk[i]
            q = p1[i + 4] - k * s - obs[i]
            q2[i] = q
            ss[i] = s * q
            a2[i + 4] = -k * q

    def stage_f(rows):
        bz = []
        z = along_z([a2[i + 4] for i in rows], w_plus[...])
        for i, dz in zip(rows, z):
            r = inv[i]
            dx = dx_plus(a2, i)
            dy = dy_plus(a2, i)
            rr[i] = dx * vx2[i + 4] + dy * vy2[i] + dz * vz2[i]
            bx[i + 4] = r * dx
            by[i] = r * dy
            bz.append(r * dz)
        for i, d in zip(rows, along_z(bz, w_minus[...])):
            zd[i] = d

    def stage_g(rows):
        for i in rows:
            q1 = q2[i] - time_ratio * (dxy_minus(bx, by, i) + zd[i])
            a1[i + 4] = -kk[i] * q1
            s = ss[i] + s1[i] * q1
            ss[i] = s
            put_grad(grad_v, i, -2.0 * time_ratio * dens[i] * speed[i] * s)

    def stage_h(rows):
        z = along_z([a1[i + 4] for i in rows], w_plus[...])
        for i, dz in zip(rows, z):
            total = rr[i] + dx_plus(a1, i) * vx1[i + 4]
            total = total + dy_plus(a1, i) * vy1[i] + dz * vz1[i]
            v = speed[i]
            put_grad(grad_r, i, inv[i] * total - time_ratio * v * v * ss[i])

    def back_line(k, slot, side):
        return remote(
            sl.at[k, slot, side], rl.at[k, slot, side], rl_s.at[k, slot, side], rl_r.at[k, slot, side],
            (line_to[side], b),
        )

    def back_z(k):
        return remote(zs.at[k], zr.at[k], rz_s.at[k], rz_r.at[k], (a, behind))

    def back_y(k):
        return remote(ys.at[k], yr.at[k], ry_s.at[k], ry_r.at[k], (a, partner))

    def term(k, slot_x, slot_y, i):
        return grads[k][block + slot_x * block - shift_x + i, pl.ds(block + slot_y * block - shift_y, block), :]

    order = (far, near, 1)

    def send_line(k):
        for slot in order:
            for side in range(2):
                @pl.when(has_line[side])
                def _():
                    def fill(i, carry):
                        sl[k, slot, side, i] = term(k, 2 * side, slot, i)
                        return carry
                    lax.fori_loop(0, block, fill, 0)
                    back_line(k, slot, side).start()

    for side in range(2):
        @pl.when(jnp.logical_not(has_line[side]))
        def _():
            for k in range(2):
                for slot in range(3):
                    rl[k, slot, 1 - side] = jnp.zeros((block, block, depth), jnp.float32)

    @pl.when(jnp.logical_not(has_onward))
    def _():
        for k in range(2):
            zr[k] = jnp.zeros((block, block, depth), jnp.float32)

    finish_halo(1)
    over(stage_b, RB_Z)
    finish_halo(0)
    over(stage_c)
    over(stage_d, RB_Z)
    over(stage_e)
    over(stage_f, RB_Z)
    over(stage_g)
    send_line(0)
    over(stage_h, RB_Z)
    send_line(1)

    def wait_line(k, slot):
        for side in range(2):
            pl.when(has_line[side])(lambda: back_line(k, slot, 1 - side).wait_recv())

    def gather(k, slot, out, extra):
        wait_line(k, slot)
        if extra is not None:
            extra[1]()
        def add(i, carry):
            total = term(k, 1, slot, i) + rl[k, slot, 0, i] + rl[k, slot, 1, i]
            if extra is not None:
                total = total + extra[0][k, i]
            out[i] = total
            return carry
        lax.fori_loop(0, block, add, 0)

    for k in range(2):
        @pl.when(has_behind)
        def _():
            gather(k, far, zs.at[k], None)
            back_z(k).start()
        @pl.when(jnp.logical_not(has_behind))
        def _():
            wait_line(k, far)
    for k in range(2):
        gather(k, near, ys.at[k], (zr, lambda: pl.when(has_onward)(lambda: back_z(k).wait_recv())))
        back_y(k).start()
    for k in range(2):
        gather(k, 1, out.at[k], (yr, lambda: back_y(k).wait_recv()))

    for k in range(2):
        fwd_y(k).wait_send()
        back_y(k).wait_send()
        pl.when(has_onward)(lambda: fwd_z(k).wait_send())
        pl.when(has_behind)(lambda: back_z(k).wait_send())
        for side in range(2):
            @pl.when(has_line[side])
            def _():
                for piece in range(2):
                    fwd_line(k, piece, side).wait_send()
                for slot in order:
                    back_line(k, slot, side).wait_send()
            pl.when(has_line[side] & has_behind)(lambda: fwd_line(k, 2, side).wait_send())


def apart(both, vel_out, rho_out):
    vel_out[...] = both[0]
    rho_out[...] = both[1]


def body(n_line, n_shot, velocity, density, start_pressure, observed, corners):
    block, _, depth = velocity.shape
    width = start_pressure.shape[0]
    cells = jax.ShapeDtypeStruct(velocity.shape, jnp.float32)

    def scratch(*shape):
        return pltpu.VMEM(shape, jnp.float32)

    along_x = scratch(width + 8, width, depth)
    plain = scratch(width, width, depth)
    extended = scratch(3 * block, 3 * block, depth)
    wide = scratch(2 * block + width, 2 * block + width, depth)
    matrix = pltpu.VMEM((2 * depth, 2 * depth), jnp.bfloat16)
    pieces = scratch(2, 3, 2, block, block, depth)
    pair = scratch(2, block, block, depth)
    sem = pltpu.SemaphoreType.DMA
    vmem = pl.BlockSpec(memory_space=pltpu.VMEM)
    both = pl.pallas_call(
        functools.partial(kernel, n_line, n_shot),
        out_shape=jax.ShapeDtypeStruct((2,) + velocity.shape, jnp.float32),
        in_specs=[pl.BlockSpec(memory_space=pltpu.SMEM)] + [vmem] * 4,
        out_specs=vmem,
        scratch_shapes=[extended] * 2 + [wide] * 2 + [along_x] * 7 + [plain] * 18
        + [matrix] * 2 + [pieces] * 2 + [pair] * 4
        + [sem((2,))] * 4 + [sem((2, 3, 2))] * 4 + [sem((2,))] * 4,
        compiler_params=pltpu.CompilerParams(
            collective_id=0, has_side_effects=True, vmem_limit_bytes=56 * 1024 * 1024
        ),
    )(corners.reshape(2), velocity, density, start_pressure, observed)
    return pl.pallas_call(
        apart, out_shape=(cells, cells), in_specs=[vmem], out_specs=(vmem, vmem)
    )(both)


def solution(mesh):
    placed = P("line", "shot", None)
    return jax.shard_map(
        functools.partial(body, mesh.shape["line"], mesh.shape["shot"]),
        mesh=mesh,
        in_specs=(placed,) * 5,
        out_specs=(placed, placed),
        check_vma=False,
    )
```

```python
import functools

import jax
import jax.numpy as jnp
import ml_dtypes
import numpy as np
from jax import lax
from jax.experimental import pallas as pl
from jax.experimental.pallas import tpu as pltpu
from jax.sharding import PartitionSpec as P

MESH = pl.DeviceIdType.MESH
coeffs = (1225.0 / 1024.0, -245.0 / 3072.0, 49.0 / 5120.0, -5.0 / 7168.0)
time_ratio = 0.1
wavelet = (20.0, -12.0)
PARTS = 2
RB = 4
RB_Z = 16


def split(value):
    high = float(np.float32(value).astype(ml_dtypes.bfloat16))
    low = float(np.float32(value - high).astype(ml_dtypes.bfloat16))
    return high, low


def band(depth, plus):
    row = lax.broadcasted_iota(jnp.int32, (depth, depth), 0)
    col = lax.broadcasted_iota(jnp.int32, (depth, depth), 1)
    gap = row - col
    high = jnp.zeros((depth, depth), jnp.float32)
    low = jnp.zeros((depth, depth), jnp.float32)
    for m in range(1, 5):
        hi, lo = split(coeffs[m - 1])
        up, down = (m, 1 - m) if plus else (m - 1, -m)
        high = jnp.where(gap == up, hi, jnp.where(gap == down, -hi, high))
        low = jnp.where(gap == up, lo, jnp.where(gap == down, -lo, low))
    top = jnp.concatenate([high, low], axis=1)
    bottom = jnp.concatenate([high, jnp.zeros_like(low)], axis=1)
    return jnp.concatenate([top, bottom], axis=0).astype(jnp.bfloat16)


def along_z(rows, matrix):
    depth = rows[0].shape[1]
    width = rows[0].shape[0]
    field = jnp.concatenate(rows, axis=0)
    high = field.astype(jnp.bfloat16)
    low = (field - high.astype(jnp.float32)).astype(jnp.bfloat16)
    both = jnp.concatenate([high, low], axis=1)
    out = jnp.dot(both, matrix, preferred_element_type=jnp.float32)
    out = out[:, :depth] + out[:, depth:]
    return [out[k * width:(k + 1) * width] for k in range(len(rows))]


def combine(pairs):
    total = None
    for c, (upper, lower) in zip(coeffs, pairs):
        term = c * (upper - lower)
        total = term if total is None else total + term
    return total


def kernel(
    n_line, n_shot,
    corner, vel_in, rho_in, p_in, obs_in,
    out,
    ext_v, ext_r, grad_v, grad_r,
    p0, p1, a2, a1, vx1, vx2, bx, vy1, vy2, by,
    ex, ey, ez, zd, inv, kk, s1, ss, q2, vz1, vz2, rr, obs, dens, speed, w_plus, w_minus,
    sl, rl, zs, zr, ys, yr,
    fy_s, fy_r, fz_s, fz_r, fl_s, fl_r, rl_s, rl_r, rz_s, rz_r, ry_s, ry_r,
):
    block, _, depth = vel_in.shape
    width = p_in.shape[0]
    a = lax.axis_index("line")
    b = lax.axis_index("shot")
    odd = lax.rem(b, 2)
    partner = b + 1 - 2 * odd
    onward = b + 2 - 4 * odd
    behind = b - 2 + 4 * odd
    has_onward = (onward >= 0) & (onward < n_shot)
    has_behind = (behind >= 0) & (behind < n_shot)
    has_line = (a > 0, a < n_line - 1)
    rows_of = block // PARTS
    chunks = [(k, h) for k in (1, 0) for h in range(PARTS)]
    back_chunks = [(k, h) for k in (0, 1) for h in range(PARTS)]
    sides = (lax.rem(a, 2), 1 - lax.rem(a, 2))
    near = 2 * (1 - odd)
    far = 2 * odd
    exts = (ext_v, ext_r)
    ins = (vel_in, rho_in)
    grads = (grad_v, grad_r)

    barrier = pltpu.get_barrier_semaphore()

    def greet(there):
        pl.semaphore_signal(barrier, inc=1, device_id=there, device_id_type=MESH)

    greet((a, partner))
    pl.when(has_onward)(lambda: greet((a, onward)))
    pl.when(has_behind)(lambda: greet((a, behind)))
    pl.when(has_line[0])(lambda: greet((a - 1, b)))
    pl.when(has_line[1])(lambda: greet((a + 1, b)))
    one = jnp.int32(1)
    none = jnp.int32(0)
    count = one
    for there in (has_onward, has_behind, has_line[0], has_line[1]):
        count = count + jnp.where(there, one, none)
    pl.semaphore_wait(barrier, count)

    def cols(slot):
        return pl.ds(pl.multiple_of(slot * block, block), block)

    def to_side(side):
        there = a - 1 + 2 * side
        return there, (there >= 0) & (there < n_line)

    def part(h, base=0):
        return pl.ds(base + h * rows_of, rows_of)

    def remote(src, dst, send, recv, there):
        return pltpu.make_async_remote_copy(
            src_ref=src, dst_ref=dst, send_sem=send, recv_sem=recv,
            device_id=there, device_id_type=MESH,
        )

    def fwd_y(k, h):
        return remote(
            ins[k].at[part(h)], exts[k].at[part(h, block), cols(far), :],
            fy_s.at[k, h], fy_r.at[k, h], (a, partner),
        )

    def fwd_z(k, h):
        return remote(
            exts[k].at[part(h, block), cols(near), :], exts[k].at[part(h, block), cols(far), :],
            fz_s.at[k, h], fz_r.at[k, h], (a, onward),
        )

    def fwd_line(k, h, piece, side):
        slot = (1, near, far)[piece]
        src = ins[k].at[part(h)] if piece == 0 else exts[k].at[part(h, block), cols(slot), :]
        dst = exts[k].at[part(h, 2 * block * (1 - side)), cols(slot), :]
        return remote(
            src, dst, fl_s.at[k, h, piece, side], fl_r.at[k, h, piece, side], (to_side(side)[0], b)
        )

    def start_line(k, h, piece):
        for side in sides:
            pl.when(to_side(side)[1])(lambda: fwd_line(k, h, piece, side).start())

    for k, h in chunks:
        fwd_y(k, h).start()
        start_line(k, h, 0)

    for k in range(2):
        exts[k][block:2 * block, block:2 * block, :] = ins[k][...]
    for field in (p0, p1, a2, a1, vx1, vx2, bx):
        field[0:4, :, :] = jnp.zeros((4, width, depth), jnp.float32)
        field[width + 4:width + 8, :, :] = jnp.zeros((4, width, depth), jnp.float32)

    turns = width // 8

    def reorder(i, carry):
        for t in range(turns):
            p0[i + 4, 8 * t:8 * t + 8, :] = p_in[i, pl.ds(t, 8, turns), :]
            obs[i, 8 * t:8 * t + 8, :] = obs_in[i, pl.ds(t, 8, turns), :]
        return carry

    lax.fori_loop(0, width, reorder, 0)
    w_plus[...] = band(depth, True)
    w_minus[...] = band(depth, False)
    wide = 2 * block + width

    def clear_grad(k):
        def clear(i, carry):
            grads[k][i] = jnp.zeros((wide, depth), jnp.float32)
            return carry
        lax.fori_loop(0, wide, clear, 0)

    def over(step, size=RB, first=0, last=width):
        def body(i, carry):
            step([i * size + k for k in range(size)])
            return carry
        lax.fori_loop(first // size, last // size, body, 0)

    sub = lax.broadcasted_iota(jnp.int32, (8, depth), 0)

    def reach(row):
        f = [row[8 * t:8 * t + 8] for t in range(turns)]
        down = [jnp.where(sub == 0, 0.0, pltpu.roll(x, 1, 0)) for x in f]
        up = [jnp.where(sub == 7, 0.0, pltpu.roll(x, 7, 0)) for x in f]
        return down + f + up

    def dx_plus(f, i):
        return combine([(f[i + 4 + m], f[i + 5 - m]) for m in range(1, 5)])

    def dy_plus(f, i):
        near_by = reach(f[i + 4])
        parts = []
        for t in range(turns, 2 * turns):
            parts.append(combine([(near_by[t + m], near_by[t + 1 - m]) for m in range(1, 5)]))
        return jnp.concatenate(parts, axis=0)

    def dxy_minus(fx, fy, i):
        near_by = reach(fy[i])
        total = None
        for m in range(1, 5):
            gap = fx[i + 3 + m] - fx[i + 4 - m]
            side = [near_by[t + m - 1] - near_by[t - m] for t in range(turns, 2 * turns)]
            term = coeffs[m - 1] * (gap + jnp.concatenate(side, axis=0))
            total = term if total is None else total + term
        return total

    def stage_a(rows):
        z = along_z([p0[i + 4] for i in rows], w_plus[...])
        for i, dz in zip(rows, z):
            ex[i] = dx_plus(p0, i)
            ey[i] = dy_plus(p0, i)
            ez[i] = dz

    def relay_near(k, h):
        fwd_y(k, h).wait_recv()
        pl.when(has_onward)(lambda: fwd_z(k, h).start())
        start_line(k, h, 1)

    def relay_far(k, h):
        @pl.when(has_behind)
        def _():
            fwd_z(k, h).wait_recv()
            start_line(k, h, 2)

    for h in range(PARTS):
        relay_near(1, h)
        if h % (PARTS // 2) == 0:
            at = h // (PARTS // 2) * (width // 2)
            over(stage_a, RB_Z, at, at + width // 2)
    for h in range(PARTS):
        relay_near(0, h)
        relay_far(1, h)
        if h % (PARTS // 2) == 0:
            clear_grad(h // (PARTS // 2))
    for h in range(PARTS):
        relay_far(0, h)

    lane = lax.broadcasted_iota(jnp.int32, (1, depth), 1)
    spot = jnp.where(lane == depth // 2, 1.0, 0.0).astype(jnp.float32)
    half = width // 2
    at = 8 * (half % turns) + half // turns
    p0[half + 4, at:at + 1, :] = p0[half + 4, at:at + 1, :] + wavelet[0] * spot
    obs[half, at:at + 1, :] = obs[half, at:at + 1, :] - wavelet[1] * spot

    def finish_halo(k):
        for piece in range(3):
            for side in range(2):
                there = has_line[side]
                if piece == 2:
                    there = there & has_behind
                for h in range(PARTS):
                    pl.when(there)(lambda: fwd_line(k, h, piece, 1 - side).wait_recv())

    shift_x = jnp.minimum(jnp.maximum(corner[0] - (a - 1) * block, 0), block)
    shift_y = jnp.minimum(jnp.maximum(corner[1] - (b - 1) * block, 0), block)

    def aperture(ext, i):
        parts = [ext[shift_x + i, pl.ds(shift_y + t, 8, turns), :] for t in range(turns)]
        return jnp.concatenate(parts, axis=0)

    def put_grad(grad, i, value):
        for t in range(turns):
            grad[i + block, pl.ds(block + t, 8, turns), :] = value[8 * t:8 * t + 8]

    def stage_b(rows):
        vz = []
        for i in rows:
            rho = aperture(ext_r, i)
            r = 1.0 / rho
            dens[i] = rho
            inv[i] = r
            t = -time_ratio * r
            vx1[i + 4] = t * ex[i]
            vy1[i] = t * ey[i]
            z = t * ez[i]
            vz1[i] = z
            vz.append(z)
        for i, d in zip(rows, along_z(vz, w_minus[...])):
            zd[i] = d

    def stage_c(rows):
        for i in rows:
            v = aperture(ext_v, i)
            k = time_ratio * dens[i] * v * v
            speed[i] = v
            s = dxy_minus(vx1, vy1, i) + zd[i]
            kk[i] = k
            s1[i] = s
            p1[i + 4] = p0[i + 4] - k * s

    def stage_d(rows):
        vz = []
        z = along_z([p1[i + 4] for i in rows], w_plus[...])
        for i, dz in zip(rows, z):
            t = -time_ratio * inv[i]
            vx2[i + 4] = vx1[i + 4] + t * dx_plus(p1, i)
            vy2[i] = vy1[i] + t * dy_plus(p1, i)
            v = vz1[i] + t * dz
            vz2[i] = v
            vz.append(v)
        for i, d in zip(rows, along_z(vz, w_minus[...])):
            zd[i] = d

    def stage_e(rows):
        for i in rows:
            s = dxy_minus(vx2, vy2, i) + zd[i]
            k = kk[i]
            q = p1[i + 4] - k * s - obs[i]
            q2[i] = q
            ss[i] = s * q
            a2[i + 4] = -k * q

    def stage_f(rows):
        bz = []
        z = along_z([a2[i + 4] for i in rows], w_plus[...])
        for i, dz in zip(rows, z):
            r = inv[i]
            dx = dx_plus(a2, i)
            dy = dy_plus(a2, i)
            rr[i] = dx * vx2[i + 4] + dy * vy2[i] + dz * vz2[i]
            bx[i + 4] = r * dx
            by[i] = r * dy
            bz.append(r * dz)
        for i, d in zip(rows, along_z(bz, w_minus[...])):
            zd[i] = d

    def stage_g(rows):
        for i in rows:
            q1 = q2[i] - time_ratio * (dxy_minus(bx, by, i) + zd[i])
            a1[i + 4] = -kk[i] * q1
            s = ss[i] + s1[i] * q1
            ss[i] = s
            put_grad(grad_v, i, -2.0 * time_ratio * dens[i] * speed[i] * s)

    def stage_h(rows):
        z = along_z([a1[i + 4] for i in rows], w_plus[...])
        for i, dz in zip(rows, z):
            total = rr[i] + dx_plus(a1, i) * vx1[i + 4]
            total = total + dy_plus(a1, i) * vy1[i] + dz * vz1[i]
            v = speed[i]
            put_grad(grad_r, i, inv[i] * total - time_ratio * v * v * ss[i])

    def back_line(k, h, slot, side):
        return remote(
            sl.at[k, slot, side, part(h)], rl.at[k, slot, side, part(h)],
            rl_s.at[k, h, slot, side], rl_r.at[k, h, slot, side], (to_side(side)[0], b),
        )

    def back_z(k, h):
        return remote(zs.at[k, part(h)], zr.at[k, part(h)], rz_s.at[k, h], rz_r.at[k, h], (a, behind))

    def back_y(k, h):
        return remote(ys.at[k, part(h)], yr.at[k, part(h)], ry_s.at[k, h], ry_r.at[k, h], (a, partner))

    def term(k, slot_x, slot_y, i):
        return grads[k][block + slot_x * block - shift_x + i, pl.ds(block + slot_y * block - shift_y, block), :]

    def send_line(k, slots):
        for slot in slots:
            for h in range(PARTS):
                for side in sides:
                    @pl.when(to_side(side)[1])
                    def _():
                        def fill(i, carry):
                            sl[k, slot, side, i] = term(k, 2 * side, slot, i)
                            return carry
                        lax.fori_loop(h * rows_of, (h + 1) * rows_of, fill, 0)
                        back_line(k, h, slot, side).start()

    for side in range(2):
        @pl.when(jnp.logical_not(has_line[side]))
        def _():
            for k in range(2):
                for slot in range(3):
                    rl[k, slot, 1 - side] = jnp.zeros((block, block, depth), jnp.float32)

    @pl.when(jnp.logical_not(has_onward))
    def _():
        for k in range(2):
            zr[k] = jnp.zeros((block, block, depth), jnp.float32)

    finish_halo(1)
    over(stage_b, RB_Z)
    finish_halo(0)
    over(stage_c)
    over(stage_d, RB_Z)
    over(stage_e)
    over(stage_f, RB_Z)
    over(stage_g)
    send_line(0, (far, near))
    over(stage_h, RB_Z)
    send_line(1, (far, near))
    send_line(0, (1,))
    send_line(1, (1,))

    def wait_line(k, h, slot):
        for side in range(2):
            pl.when(has_line[side])(lambda: back_line(k, h, slot, 1 - side).wait_recv())

    def gather(k, h, slot, out, extra):
        wait_line(k, h, slot)
        if extra is not None:
            extra[1]()
        def add(i, carry):
            total = term(k, 1, slot, i) + rl[k, slot, 0, i] + rl[k, slot, 1, i]
            if extra is not None:
                total = total + extra[0][k, i]
            out[k, i] = total
            return carry
        lax.fori_loop(h * rows_of, (h + 1) * rows_of, add, 0)

    for k, h in back_chunks:
        @pl.when(has_behind)
        def _():
            gather(k, h, far, zs, None)
            back_z(k, h).start()
        @pl.when(jnp.logical_not(has_behind))
        def _():
            wait_line(k, h, far)
    for k, h in back_chunks:
        gather(k, h, near, ys, (zr, lambda: pl.when(has_onward)(lambda: back_z(k, h).wait_recv())))
        back_y(k, h).start()
    for k, h in back_chunks:
        gather(k, h, 1, out, (yr, lambda: back_y(k, h).wait_recv()))

    for k, h in chunks:
        fwd_y(k, h).wait_send()
        back_y(k, h).wait_send()
        pl.when(has_onward)(lambda: fwd_z(k, h).wait_send())
        pl.when(has_behind)(lambda: back_z(k, h).wait_send())
        for side in range(2):
            @pl.when(has_line[side])
            def _():
                for piece in range(2):
                    fwd_line(k, h, piece, side).wait_send()
                for slot in range(3):
                    back_line(k, h, slot, side).wait_send()
            pl.when(has_line[side] & has_behind)(lambda: fwd_line(k, h, 2, side).wait_send())


def apart(both, vel_out, rho_out):
    vel_out[...] = both[0]
    rho_out[...] = both[1]


def body(n_line, n_shot, velocity, density, start_pressure, observed, corners):
    block, _, depth = velocity.shape
    width = start_pressure.shape[0]
    cells = jax.ShapeDtypeStruct(velocity.shape, jnp.float32)

    def scratch(*shape):
        return pltpu.VMEM(shape, jnp.float32)

    along_x = scratch(width + 8, width, depth)
    plain = scratch(width, width, depth)
    extended = scratch(3 * block, 3 * block, depth)
    wide = scratch(2 * block + width, 2 * block + width, depth)
    matrix = pltpu.VMEM((2 * depth, 2 * depth), jnp.bfloat16)
    pieces = scratch(2, 3, 2, block, block, depth)
    pair = scratch(2, block, block, depth)
    sem = pltpu.SemaphoreType.DMA
    vmem = pl.BlockSpec(memory_space=pltpu.VMEM)
    both = pl.pallas_call(
        functools.partial(kernel, n_line, n_shot),
        out_shape=jax.ShapeDtypeStruct((2,) + velocity.shape, jnp.float32),
        in_specs=[pl.BlockSpec(memory_space=pltpu.SMEM)] + [vmem] * 4,
        out_specs=vmem,
        scratch_shapes=[extended] * 2 + [wide] * 2 + [along_x] * 7 + [plain] * 18
        + [matrix] * 2 + [pieces] * 2 + [pair] * 4
        + [sem((2, PARTS))] * 4 + [sem((2, PARTS, 3, 2))] * 4 + [sem((2, PARTS))] * 4,
        compiler_params=pltpu.CompilerParams(
            collective_id=0, has_side_effects=True, vmem_limit_bytes=56 * 1024 * 1024
        ),
    )(corners.reshape(2), velocity, density, start_pressure, observed)
    return pl.pallas_call(
        apart, out_shape=(cells, cells), in_specs=[vmem], out_specs=(vmem, vmem)
    )(both)


def solution(mesh):
    placed = P("line", "shot", None)
    return jax.shard_map(
        functools.partial(body, mesh.shape["line"], mesh.shape["shot"]),
        mesh=mesh,
        in_specs=(placed,) * 5,
        out_specs=(placed, placed),
        check_vma=False,
    )
```

```python
import functools

import jax
import jax.numpy as jnp
import ml_dtypes
import numpy as np
from jax import lax
from jax.experimental import pallas as pl
from jax.experimental.pallas import tpu as pltpu
from jax.sharding import PartitionSpec as P

MESH = pl.DeviceIdType.MESH
coeffs = (1225.0 / 1024.0, -245.0 / 3072.0, 49.0 / 5120.0, -5.0 / 7168.0)
time_ratio = 0.1
wavelet = (20.0, -12.0)
PARTS = 2
RB = 4
RB_Z = 16


def split(value):
    high = float(np.float32(value).astype(ml_dtypes.bfloat16))
    low = float(np.float32(value - high).astype(ml_dtypes.bfloat16))
    return high, low


def band(depth, plus):
    row = lax.broadcasted_iota(jnp.int32, (depth, depth), 0)
    col = lax.broadcasted_iota(jnp.int32, (depth, depth), 1)
    gap = row - col
    high = jnp.zeros((depth, depth), jnp.float32)
    low = jnp.zeros((depth, depth), jnp.float32)
    for m in range(1, 5):
        hi, lo = split(coeffs[m - 1])
        up, down = (m, 1 - m) if plus else (m - 1, -m)
        high = jnp.where(gap == up, hi, jnp.where(gap == down, -hi, high))
        low = jnp.where(gap == up, lo, jnp.where(gap == down, -lo, low))
    top = jnp.concatenate([high, low], axis=1)
    bottom = jnp.concatenate([high, jnp.zeros_like(low)], axis=1)
    return jnp.concatenate([top, bottom], axis=0).astype(jnp.bfloat16)


def along_z(rows, matrix):
    depth = rows[0].shape[1]
    width = rows[0].shape[0]
    field = jnp.concatenate(rows, axis=0)
    high = field.astype(jnp.bfloat16)
    low = (field - high.astype(jnp.float32)).astype(jnp.bfloat16)
    both = jnp.concatenate([high, low], axis=1)
    out = jnp.dot(both, matrix, preferred_element_type=jnp.float32)
    out = out[:, :depth] + out[:, depth:]
    return [out[k * width:(k + 1) * width] for k in range(len(rows))]


def combine(pairs):
    total = None
    for c, (upper, lower) in zip(coeffs, pairs):
        term = c * (upper - lower)
        total = term if total is None else total + term
    return total


def kernel(
    n_line, n_shot,
    corner, vel_in, rho_in, p_in, obs_in,
    out,
    ext_v, ext_r, grad_v, grad_r,
    p0, p1, a2, a1, vx1, vx2, bx, vy1, vy2, by,
    ex, ey, ez, zd, inv, kk, s1, ss, q2, vz1, vz2, rr, obs, dens, speed, w_plus, w_minus,
    cs, sl, rl, zs, zr, ys, yr, place, places,
    fy_s, fy_r, fz_s, fz_r, fl_s, fl_r, rl_s, rl_r, rz_s, rz_r, ry_s, ry_r, at_s, at_r,
):
    block, _, depth = vel_in.shape
    width = p_in.shape[0]
    a = lax.axis_index("line")
    b = lax.axis_index("shot")
    odd = lax.rem(b, 2)
    partner = b + 1 - 2 * odd
    onward = b + 2 - 4 * odd
    behind = b - 2 + 4 * odd
    has_onward = (onward >= 0) & (onward < n_shot)
    has_behind = (behind >= 0) & (behind < n_shot)
    has_line = (a > 0, a < n_line - 1)
    rows_of = block // PARTS
    chunks = [(k, h) for k in (1, 0) for h in range(PARTS)]
    back_chunks = [(k, h) for k in (0, 1) for h in range(PARTS)]
    sides = (lax.rem(a, 2), 1 - lax.rem(a, 2))
    near = 2 * (1 - odd)
    far = 2 * odd
    exts = (ext_v, ext_r)
    ins = (vel_in, rho_in)
    grads = (grad_v, grad_r)

    barrier = pltpu.get_barrier_semaphore()

    def greet(there):
        pl.semaphore_signal(barrier, inc=1, device_id=there, device_id_type=MESH)

    greet((a, partner))
    pl.when(has_onward)(lambda: greet((a, onward)))
    pl.when(has_behind)(lambda: greet((a, behind)))
    pl.when(has_line[0])(lambda: greet((a - 1, b)))
    pl.when(has_line[1])(lambda: greet((a + 1, b)))
    one = jnp.int32(1)
    none = jnp.int32(0)
    count = one
    for there in (has_onward, has_behind, has_line[0], has_line[1]):
        count = count + jnp.where(there, one, none)
    pl.semaphore_wait(barrier, count)

    def cols(slot):
        return pl.ds(pl.multiple_of(slot * block, block), block)

    def to_side(side):
        there = a - 1 + 2 * side
        return there, (there >= 0) & (there < n_line)

    def part(h, base=0):
        return pl.ds(base + h * rows_of, rows_of)

    def remote(src, dst, send, recv, there):
        return pltpu.make_async_remote_copy(
            src_ref=src, dst_ref=dst, send_sem=send, recv_sem=recv,
            device_id=there, device_id_type=MESH,
        )

    def fwd_y(k, h):
        return remote(
            ins[k].at[part(h)], exts[k].at[part(h, block), cols(far), :],
            fy_s.at[k, h], fy_r.at[k, h], (a, partner),
        )

    def fwd_z(k, h):
        return remote(
            exts[k].at[part(h, block), cols(near), :], exts[k].at[part(h, block), cols(far), :],
            fz_s.at[k, h], fz_r.at[k, h], (a, onward),
        )

    def fwd_line(k, h, piece, side):
        src = ins[k].at[part(h)] if piece == 0 else cs.at[k, side, part(h)]
        dst = exts[k].at[part(h, 2 * block * (1 - side)), cols(1 - piece), :]
        return remote(
            src, dst, fl_s.at[k, h, piece, side], fl_r.at[k, h, piece, side], (to_side(side)[0], b)
        )

    def start_line(k, h, piece):
        for side in sides:
            pl.when(to_side(side)[1])(lambda: fwd_line(k, h, piece, side).start())

    def tell(side):
        return remote(
            place, places.at[1 - side], at_s.at[side], at_r.at[1 - side], (to_side(side)[0], b)
        )

    shift_x = jnp.minimum(jnp.maximum(corner[0] - (a - 1) * block, 0), block)
    shift_y = jnp.minimum(jnp.maximum(corner[1] - (b - 1) * block, 0), block)
    place[...] = jnp.zeros((8, depth), jnp.int32) + shift_y
    for side in range(2):
        pl.when(has_line[side])(lambda: tell(side).start())

        @pl.when(jnp.logical_not(has_line[side]))
        def _():
            places[side] = jnp.zeros((8, depth), jnp.int32)

    for k, h in chunks:
        fwd_y(k, h).start()
        start_line(k, h, 0)

    for k in range(2):
        exts[k][block:2 * block, block:2 * block, :] = ins[k][...]
    for field in (p0, p1, a2, a1, vx1, vx2, bx):
        field[0:4, :, :] = jnp.zeros((4, width, depth), jnp.float32)
        field[width + 4:width + 8, :, :] = jnp.zeros((4, width, depth), jnp.float32)

    turns = width // 8

    def reorder(i, carry):
        for t in range(turns):
            p0[i + 4, 8 * t:8 * t + 8, :] = p_in[i, pl.ds(t, 8, turns), :]
            obs[i, 8 * t:8 * t + 8, :] = obs_in[i, pl.ds(t, 8, turns), :]
        return carry

    lax.fori_loop(0, width, reorder, 0)
    w_plus[...] = band(depth, True)
    w_minus[...] = band(depth, False)
    wide = 2 * block + width

    def clear_grad(k):
        def clear(i, carry):
            grads[k][i] = jnp.zeros((wide, depth), jnp.float32)
            return carry
        lax.fori_loop(0, wide, clear, 0)

    def over(step, size=RB, first=0, last=width):
        def body(i, carry):
            step([i * size + k for k in range(size)])
            return carry
        lax.fori_loop(first // size, last // size, body, 0)

    sub = lax.broadcasted_iota(jnp.int32, (8, depth), 0)

    def reach(row):
        f = [row[8 * t:8 * t + 8] for t in range(turns)]
        down = [jnp.where(sub == 0, 0.0, pltpu.roll(x, 1, 0)) for x in f]
        up = [jnp.where(sub == 7, 0.0, pltpu.roll(x, 7, 0)) for x in f]
        return down + f + up

    def dx_plus(f, i):
        return combine([(f[i + 4 + m], f[i + 5 - m]) for m in range(1, 5)])

    def dy_plus(f, i):
        near_by = reach(f[i + 4])
        parts = []
        for t in range(turns, 2 * turns):
            parts.append(combine([(near_by[t + m], near_by[t + 1 - m]) for m in range(1, 5)]))
        return jnp.concatenate(parts, axis=0)

    def dxy_minus(fx, fy, i):
        near_by = reach(fy[i])
        total = None
        for m in range(1, 5):
            gap = fx[i + 3 + m] - fx[i + 4 - m]
            side = [near_by[t + m - 1] - near_by[t - m] for t in range(turns, 2 * turns)]
            term = coeffs[m - 1] * (gap + jnp.concatenate(side, axis=0))
            total = term if total is None else total + term
        return total

    def stage_a(rows):
        z = along_z([p0[i + 4] for i in rows], w_plus[...])
        for i, dz in zip(rows, z):
            ex[i] = dx_plus(p0, i)
            ey[i] = dy_plus(p0, i)
            ez[i] = dz

    def relay_near(k, h):
        fwd_y(k, h).wait_recv()
        pl.when(has_onward)(lambda: fwd_z(k, h).start())

    column = lax.broadcasted_iota(jnp.int32, (8, depth), 0)

    def relay_far(k, h):
        pl.when(has_behind)(lambda: fwd_z(k, h).wait_recv())
        for side in sides:
            @pl.when(to_side(side)[1])
            def _():
                start = places[side]
                def fill(i, carry):
                    for c in range(0, block, 8):
                        left = exts[k][block + i, c:c + 8, :]
                        right = exts[k][block + i, 2 * block + c:2 * block + c + 8, :]
                        cs[k, side, i, c:c + 8, :] = jnp.where(column + c >= start, left, right)
                    return carry
                lax.fori_loop(h * rows_of, (h + 1) * rows_of, fill, 0)
                fwd_line(k, h, 1, side).start()

    for side in range(2):
        pl.when(has_line[side])(lambda: tell(1 - side).wait_recv())

    for h in range(PARTS):
        relay_near(1, h)
        if h % (PARTS // 2) == 0:
            at = h // (PARTS // 2) * (width // 2)
            over(stage_a, RB_Z, at, at + width // 2)
    for h in range(PARTS):
        relay_near(0, h)
        relay_far(1, h)
        if h % (PARTS // 2) == 0:
            clear_grad(h // (PARTS // 2))
    for h in range(PARTS):
        relay_far(0, h)

    lane = lax.broadcasted_iota(jnp.int32, (1, depth), 1)
    spot = jnp.where(lane == depth // 2, 1.0, 0.0).astype(jnp.float32)
    half = width // 2
    at = 8 * (half % turns) + half // turns
    p0[half + 4, at:at + 1, :] = p0[half + 4, at:at + 1, :] + wavelet[0] * spot
    obs[half, at:at + 1, :] = obs[half, at:at + 1, :] - wavelet[1] * spot

    def finish_halo(k):
        for side in range(2):
            @pl.when(has_line[side])
            def _():
                for piece in range(2):
                    for h in range(PARTS):
                        fwd_line(k, h, piece, 1 - side).wait_recv()
                first = 2 * block * side
                def both(i, carry):
                    exts[k][first + i, 2 * block:3 * block, :] = exts[k][first + i, 0:block, :]
                    return carry
                lax.fori_loop(0, block, both, 0)

    def aperture(ext, i):
        parts = [ext[shift_x + i, pl.ds(shift_y + t, 8, turns), :] for t in range(turns)]
        return jnp.concatenate(parts, axis=0)

    def put_grad(grad, i, value):
        for t in range(turns):
            grad[i + block, pl.ds(block + t, 8, turns), :] = value[8 * t:8 * t + 8]

    def stage_b(rows):
        vz = []
        for i in rows:
            rho = aperture(ext_r, i)
            r = 1.0 / rho
            dens[i] = rho
            inv[i] = r
            t = -time_ratio * r
            vx1[i + 4] = t * ex[i]
            vy1[i] = t * ey[i]
            z = t * ez[i]
            vz1[i] = z
            vz.append(z)
        for i, d in zip(rows, along_z(vz, w_minus[...])):
            zd[i] = d

    def stage_c(rows):
        for i in rows:
            v = aperture(ext_v, i)
            k = time_ratio * dens[i] * v * v
            speed[i] = v
            s = dxy_minus(vx1, vy1, i) + zd[i]
            kk[i] = k
            s1[i] = s
            p1[i + 4] = p0[i + 4] - k * s

    def stage_d(rows):
        vz = []
        z = along_z([p1[i + 4] for i in rows], w_plus[...])
        for i, dz in zip(rows, z):
            t = -time_ratio * inv[i]
            vx2[i + 4] = vx1[i + 4] + t * dx_plus(p1, i)
            vy2[i] = vy1[i] + t * dy_plus(p1, i)
            v = vz1[i] + t * dz
            vz2[i] = v
            vz.append(v)
        for i, d in zip(rows, along_z(vz, w_minus[...])):
            zd[i] = d

    def stage_e(rows):
        for i in rows:
            s = dxy_minus(vx2, vy2, i) + zd[i]
            k = kk[i]
            q = p1[i + 4] - k * s - obs[i]
            q2[i] = q
            ss[i] = s * q
            a2[i + 4] = -k * q

    def stage_f(rows):
        bz = []
        z = along_z([a2[i + 4] for i in rows], w_plus[...])
        for i, dz in zip(rows, z):
            r = inv[i]
            dx = dx_plus(a2, i)
            dy = dy_plus(a2, i)
            rr[i] = dx * vx2[i + 4] + dy * vy2[i] + dz * vz2[i]
            bx[i + 4] = r * dx
            by[i] = r * dy
            bz.append(r * dz)
        for i, d in zip(rows, along_z(bz, w_minus[...])):
            zd[i] = d

    def stage_g(rows):
        for i in rows:
            q1 = q2[i] - time_ratio * (dxy_minus(bx, by, i) + zd[i])
            a1[i + 4] = -kk[i] * q1
            s = ss[i] + s1[i] * q1
            ss[i] = s
            put_grad(grad_v, i, -2.0 * time_ratio * dens[i] * speed[i] * s)

    def stage_h(rows):
        z = along_z([a1[i + 4] for i in rows], w_plus[...])
        for i, dz in zip(rows, z):
            total = rr[i] + dx_plus(a1, i) * vx1[i + 4]
            total = total + dy_plus(a1, i) * vy1[i] + dz * vz1[i]
            v = speed[i]
            put_grad(grad_r, i, inv[i] * total - time_ratio * v * v * ss[i])

    def back_line(k, h, piece, side):
        return remote(
            sl.at[k, piece, side, part(h)], rl.at[k, piece, side, part(h)],
            rl_s.at[k, h, piece, side], rl_r.at[k, h, piece, side], (to_side(side)[0], b),
        )

    def back_z(k, h):
        return remote(zs.at[k, part(h)], zr.at[k, part(h)], rz_s.at[k, h], rz_r.at[k, h], (a, behind))

    def back_y(k, h):
        return remote(ys.at[k, part(h)], yr.at[k, part(h)], ry_s.at[k, h], ry_r.at[k, h], (a, partner))

    def term(k, slot_x, slot_y, i):
        return grads[k][block + slot_x * block - shift_x + i, pl.ds(block + slot_y * block - shift_y, block), :]

    def send_line(k, piece):
        for h in range(PARTS):
            for side in sides:
                @pl.when(to_side(side)[1])
                def _():
                    def fill(i, carry):
                        if piece == 0:
                            sl[k, 0, side, i] = term(k, 2 * side, 1, i)
                        else:
                            sl[k, 1, side, i] = term(k, 2 * side, 0, i) + term(k, 2 * side, 2, i)
                        return carry
                    lax.fori_loop(h * rows_of, (h + 1) * rows_of, fill, 0)
                    back_line(k, h, piece, side).start()

    for side in range(2):
        @pl.when(jnp.logical_not(has_line[side]))
        def _():
            for k in range(2):
                for piece in range(2):
                    rl[k, piece, 1 - side] = jnp.zeros((block, block, depth), jnp.float32)

    @pl.when(jnp.logical_not(has_onward))
    def _():
        for k in range(2):
            zr[k] = jnp.zeros((block, block, depth), jnp.float32)

    finish_halo(1)
    over(stage_b, RB_Z)
    finish_halo(0)
    over(stage_c)
    over(stage_d, RB_Z)
    over(stage_e)
    over(stage_f, RB_Z)
    over(stage_g)
    send_line(0, 1)
    over(stage_h, RB_Z)
    send_line(1, 1)
    send_line(0, 0)
    send_line(1, 0)

    def wait_line(k, h, piece):
        for side in range(2):
            pl.when(has_line[side])(lambda: back_line(k, h, piece, 1 - side).wait_recv())

    def gather(k, h, slot, out, extra):
        def add(i, carry):
            for c in range(0, block, 8):
                cells = pl.ds(c, 8)
                total = grads[k][
                    2 * block - shift_x + i, pl.ds(block + slot * block - shift_y + c, 8), :
                ]
                for side in range(2):
                    if isinstance(slot, int):
                        total = total + rl[k, 0, 1 - side, i, cells, :]
                    else:
                        inside = (column + c - places[side]) * (1 - slot) - slot // 2 >= 0
                        total = total + jnp.where(inside, rl[k, 1, 1 - side, i, cells, :], 0.0)
                if extra is not None:
                    total = total + extra[k, i, cells, :]
                out[k, i, cells, :] = total
            return carry
        lax.fori_loop(h * rows_of, (h + 1) * rows_of, add, 0)

    for k, h in back_chunks:
        wait_line(k, h, 1)
        @pl.when(has_behind)
        def _():
            gather(k, h, far, zs, None)
            back_z(k, h).start()
    for k, h in back_chunks:
        pl.when(has_onward)(lambda: back_z(k, h).wait_recv())
        gather(k, h, near, ys, zr)
        back_y(k, h).start()
    for k, h in back_chunks:
        wait_line(k, h, 0)
        back_y(k, h).wait_recv()
        gather(k, h, 1, out, yr)

    for k, h in chunks:
        fwd_y(k, h).wait_send()
        back_y(k, h).wait_send()
        pl.when(has_onward)(lambda: fwd_z(k, h).wait_send())
        pl.when(has_behind)(lambda: back_z(k, h).wait_send())
        for side in range(2):
            @pl.when(has_line[side])
            def _():
                for piece in range(2):
                    fwd_line(k, h, piece, side).wait_send()
                    back_line(k, h, piece, side).wait_send()
    for side in range(2):
        pl.when(has_line[side])(lambda: tell(side).wait_send())


def apart(both, vel_out, rho_out):
    vel_out[...] = both[0]
    rho_out[...] = both[1]


def body(n_line, n_shot, velocity, density, start_pressure, observed, corners):
    block, _, depth = velocity.shape
    width = start_pressure.shape[0]
    cells = jax.ShapeDtypeStruct(velocity.shape, jnp.float32)

    def scratch(*shape):
        return pltpu.VMEM(shape, jnp.float32)

    along_x = scratch(width + 8, width, depth)
    plain = scratch(width, width, depth)
    extended = scratch(3 * block, 3 * block, depth)
    wide = scratch(2 * block + width, 2 * block + width, depth)
    matrix = pltpu.VMEM((2 * depth, 2 * depth), jnp.bfloat16)
    pieces = scratch(2, 2, 2, block, block, depth)
    place = pltpu.VMEM((8, depth), jnp.int32)
    places = pltpu.VMEM((2, 8, depth), jnp.int32)
    pair = scratch(2, block, block, depth)
    sem = pltpu.SemaphoreType.DMA
    vmem = pl.BlockSpec(memory_space=pltpu.VMEM)
    both = pl.pallas_call(
        functools.partial(kernel, n_line, n_shot),
        out_shape=jax.ShapeDtypeStruct((2,) + velocity.shape, jnp.float32),
        in_specs=[pl.BlockSpec(memory_space=pltpu.SMEM)] + [vmem] * 4,
        out_specs=vmem,
        scratch_shapes=[extended] * 2 + [wide] * 2 + [along_x] * 7 + [plain] * 18
        + [matrix] * 2 + [scratch(2, 2, block, block, depth)] + [pieces] * 2 + [pair] * 4 + [place, places]
        + [sem((2, PARTS))] * 4 + [sem((2, PARTS, 2, 2))] * 4 + [sem((2, PARTS))] * 4 + [sem((2,))] * 2,
        compiler_params=pltpu.CompilerParams(
            collective_id=0, has_side_effects=True, vmem_limit_bytes=56 * 1024 * 1024
        ),
    )(corners.reshape(2), velocity, density, start_pressure, observed)
    return pl.pallas_call(
        apart, out_shape=(cells, cells), in_specs=[vmem], out_specs=(vmem, vmem)
    )(both)


def solution(mesh):
    placed = P("line", "shot", None)
    return jax.shard_map(
        functools.partial(body, mesh.shape["line"], mesh.shape["shot"]),
        mesh=mesh,
        in_specs=(placed,) * 5,
        out_specs=(placed, placed),
        check_vma=False,
    )
```

```python
import functools

import jax
import jax.numpy as jnp
import ml_dtypes
import numpy as np
from jax import lax
from jax.experimental import pallas as pl
from jax.experimental.pallas import tpu as pltpu
from jax.sharding import PartitionSpec as P

MESH = pl.DeviceIdType.MESH
coeffs = (1225.0 / 1024.0, -245.0 / 3072.0, 49.0 / 5120.0, -5.0 / 7168.0)
time_ratio = 0.1
wavelet = (20.0, -12.0)
PARTS = 4
RB = 4
RB_Z = 16


def split(value):
    high = float(np.float32(value).astype(ml_dtypes.bfloat16))
    low = float(np.float32(value - high).astype(ml_dtypes.bfloat16))
    return high, low


def band(depth, plus):
    row = lax.broadcasted_iota(jnp.int32, (depth, depth), 0)
    col = lax.broadcasted_iota(jnp.int32, (depth, depth), 1)
    gap = row - col
    high = jnp.zeros((depth, depth), jnp.float32)
    low = jnp.zeros((depth, depth), jnp.float32)
    for m in range(1, 5):
        hi, lo = split(coeffs[m - 1])
        up, down = (m, 1 - m) if plus else (m - 1, -m)
        high = jnp.where(gap == up, hi, jnp.where(gap == down, -hi, high))
        low = jnp.where(gap == up, lo, jnp.where(gap == down, -lo, low))
    top = jnp.concatenate([high, low], axis=1)
    bottom = jnp.concatenate([high, jnp.zeros_like(low)], axis=1)
    return jnp.concatenate([top, bottom], axis=0).astype(jnp.bfloat16)


def along_z(rows, matrix):
    depth = rows[0].shape[1]
    width = rows[0].shape[0]
    field = jnp.concatenate(rows, axis=0)
    high = field.astype(jnp.bfloat16)
    low = (field - high.astype(jnp.float32)).astype(jnp.bfloat16)
    both = jnp.concatenate([high, low], axis=1)
    out = jnp.dot(both, matrix, preferred_element_type=jnp.float32)
    out = out[:, :depth] + out[:, depth:]
    return [out[k * width:(k + 1) * width] for k in range(len(rows))]


def combine(pairs):
    total = None
    for c, (upper, lower) in zip(coeffs, pairs):
        term = c * (upper - lower)
        total = term if total is None else total + term
    return total


def kernel(
    n_line, n_shot,
    corner, vel_in, rho_in, p_in, obs_in,
    out,
    ext_v, ext_r, grad_v, grad_r,
    p0, p1, a2, a1, vx1, vx2, bx, vy1, vy2, by,
    ex, ey, ez, zd, inv, kk, s1, ss, q2, vz1, vz2, rr, obs, dens, speed, w_plus, w_minus,
    cs, sl, rl, zs, zr, ys, yr, place, places,
    fy_s, fy_r, fz_s, fz_r, fl_s, fl_r, rl_s, rl_r, rz_s, rz_r, ry_s, ry_r, at_s, at_r,
):
    block, _, depth = vel_in.shape
    width = p_in.shape[0]
    a = lax.axis_index("line")
    b = lax.axis_index("shot")
    odd = lax.rem(b, 2)
    partner = b + 1 - 2 * odd
    onward = b + 2 - 4 * odd
    behind = b - 2 + 4 * odd
    has_onward = (onward >= 0) & (onward < n_shot)
    has_behind = (behind >= 0) & (behind < n_shot)
    has_line = (a > 0, a < n_line - 1)
    rows_of = block // PARTS
    chunks = [(k, h) for k in (1, 0) for h in range(PARTS)]
    back_chunks = [(k, h) for k in (0, 1) for h in range(PARTS)]
    sides = (lax.rem(a, 2), 1 - lax.rem(a, 2))
    near = 2 * (1 - odd)
    far = 2 * odd
    exts = (ext_v, ext_r)
    ins = (vel_in, rho_in)
    grads = (grad_v, grad_r)

    barrier = pltpu.get_barrier_semaphore()

    def greet(there):
        pl.semaphore_signal(barrier, inc=1, device_id=there, device_id_type=MESH)

    greet((a, partner))
    pl.when(has_onward)(lambda: greet((a, onward)))
    pl.when(has_behind)(lambda: greet((a, behind)))
    pl.when(has_line[0])(lambda: greet((a - 1, b)))
    pl.when(has_line[1])(lambda: greet((a + 1, b)))
    one = jnp.int32(1)
    none = jnp.int32(0)
    count = one
    for there in (has_onward, has_behind, has_line[0], has_line[1]):
        count = count + jnp.where(there, one, none)
    pl.semaphore_wait(barrier, count)

    def cols(slot):
        return pl.ds(pl.multiple_of(slot * block, block), block)

    def to_side(side):
        there = a - 1 + 2 * side
        return there, (there >= 0) & (there < n_line)

    def part(h, base=0):
        return pl.ds(base + h * rows_of, rows_of)

    def remote(src, dst, send, recv, there):
        return pltpu.make_async_remote_copy(
            src_ref=src, dst_ref=dst, send_sem=send, recv_sem=recv,
            device_id=there, device_id_type=MESH,
        )

    def fwd_y(k, h):
        return remote(
            ins[k].at[part(h)], exts[k].at[part(h, block), cols(far), :],
            fy_s.at[k, h], fy_r.at[k, h], (a, partner),
        )

    def fwd_z(k, h):
        return remote(
            exts[k].at[part(h, block), cols(near), :], exts[k].at[part(h, block), cols(far), :],
            fz_s.at[k, h], fz_r.at[k, h], (a, onward),
        )

    def fwd_line(k, h, piece, side):
        src = ins[k].at[part(h)] if piece == 0 else cs.at[k, side, part(h)]
        dst = exts[k].at[part(h, 2 * block * (1 - side)), cols(1 - piece), :]
        return remote(
            src, dst, fl_s.at[k, h, piece, side], fl_r.at[k, h, piece, side], (to_side(side)[0], b)
        )

    def start_line(k, h, piece):
        for side in sides:
            pl.when(to_side(side)[1])(lambda: fwd_line(k, h, piece, side).start())

    def tell(side):
        return remote(
            place, places.at[1 - side], at_s.at[side], at_r.at[1 - side], (to_side(side)[0], b)
        )

    shift_x = jnp.minimum(jnp.maximum(corner[0] - (a - 1) * block, 0), block)
    shift_y = jnp.minimum(jnp.maximum(corner[1] - (b - 1) * block, 0), block)
    place[...] = jnp.zeros((8, depth), jnp.int32) + shift_y
    for side in range(2):
        pl.when(has_line[side])(lambda: tell(side).start())

        @pl.when(jnp.logical_not(has_line[side]))
        def _():
            places[side] = jnp.zeros((8, depth), jnp.int32)

    for k, h in chunks:
        fwd_y(k, h).start()
        start_line(k, h, 0)

    for k in range(2):
        exts[k][block:2 * block, block:2 * block, :] = ins[k][...]
    for field in (p0, p1, a2, a1, vx1, vx2, bx):
        field[0:4, :, :] = jnp.zeros((4, width, depth), jnp.float32)
        field[width + 4:width + 8, :, :] = jnp.zeros((4, width, depth), jnp.float32)

    turns = width // 8

    def reorder(i, carry):
        for t in range(turns):
            p0[i + 4, 8 * t:8 * t + 8, :] = p_in[i, pl.ds(t, 8, turns), :]
            obs[i, 8 * t:8 * t + 8, :] = obs_in[i, pl.ds(t, 8, turns), :]
        return carry

    lax.fori_loop(0, width, reorder, 0)
    w_plus[...] = band(depth, True)
    w_minus[...] = band(depth, False)
    wide = 2 * block + width

    def clear_grad(k):
        def clear(i, carry):
            grads[k][i] = jnp.zeros((wide, depth), jnp.float32)
            return carry
        lax.fori_loop(0, wide, clear, 0)

    def over(step, size=RB, first=0, last=width):
        def body(i, carry):
            step([i * size + k for k in range(size)])
            return carry
        lax.fori_loop(first // size, last // size, body, 0)

    sub = lax.broadcasted_iota(jnp.int32, (8, depth), 0)

    def reach(row):
        f = [row[8 * t:8 * t + 8] for t in range(turns)]
        down = [jnp.where(sub == 0, 0.0, pltpu.roll(x, 1, 0)) for x in f]
        up = [jnp.where(sub == 7, 0.0, pltpu.roll(x, 7, 0)) for x in f]
        return down + f + up

    def dx_plus(f, i):
        return combine([(f[i + 4 + m], f[i + 5 - m]) for m in range(1, 5)])

    def dy_plus(f, i):
        near_by = reach(f[i + 4])
        parts = []
        for t in range(turns, 2 * turns):
            parts.append(combine([(near_by[t + m], near_by[t + 1 - m]) for m in range(1, 5)]))
        return jnp.concatenate(parts, axis=0)

    def dxy_minus(fx, fy, i):
        near_by = reach(fy[i])
        total = None
        for m in range(1, 5):
            gap = fx[i + 3 + m] - fx[i + 4 - m]
            side = [near_by[t + m - 1] - near_by[t - m] for t in range(turns, 2 * turns)]
            term = coeffs[m - 1] * (gap + jnp.concatenate(side, axis=0))
            total = term if total is None else total + term
        return total

    def stage_a(rows):
        z = along_z([p0[i + 4] for i in rows], w_plus[...])
        for i, dz in zip(rows, z):
            ex[i] = dx_plus(p0, i)
            ey[i] = dy_plus(p0, i)
            ez[i] = dz

    def relay_near(k, h):
        fwd_y(k, h).wait_recv()
        pl.when(has_onward)(lambda: fwd_z(k, h).start())

    column = lax.broadcasted_iota(jnp.int32, (8, depth), 0)

    def relay_far(k, h):
        pl.when(has_behind)(lambda: fwd_z(k, h).wait_recv())
        for side in sides:
            @pl.when(to_side(side)[1])
            def _():
                start = places[side]
                def fill(i, carry):
                    for c in range(0, block, 8):
                        left = exts[k][block + i, c:c + 8, :]
                        right = exts[k][block + i, 2 * block + c:2 * block + c + 8, :]
                        cs[k, side, i, c:c + 8, :] = jnp.where(column + c >= start, left, right)
                    return carry
                lax.fori_loop(h * rows_of, (h + 1) * rows_of, fill, 0)
                fwd_line(k, h, 1, side).start()

    for side in range(2):
        pl.when(has_line[side])(lambda: tell(1 - side).wait_recv())

    for h in range(PARTS):
        relay_near(1, h)
        if h % (PARTS // 2) == 0:
            at = h // (PARTS // 2) * (width // 2)
            over(stage_a, RB_Z, at, at + width // 2)
    for h in range(PARTS):
        relay_near(0, h)
        relay_far(1, h)
        if h % (PARTS // 2) == 0:
            clear_grad(h // (PARTS // 2))
    for h in range(PARTS):
        relay_far(0, h)

    lane = lax.broadcasted_iota(jnp.int32, (1, depth), 1)
    spot = jnp.where(lane == depth // 2, 1.0, 0.0).astype(jnp.float32)
    half = width // 2
    at = 8 * (half % turns) + half // turns
    p0[half + 4, at:at + 1, :] = p0[half + 4, at:at + 1, :] + wavelet[0] * spot
    obs[half, at:at + 1, :] = obs[half, at:at + 1, :] - wavelet[1] * spot

    def finish_halo(k):
        for side in range(2):
            @pl.when(has_line[side])
            def _():
                for piece in range(2):
                    for h in range(PARTS):
                        fwd_line(k, h, piece, 1 - side).wait_recv()
                first = 2 * block * side
                def both(i, carry):
                    exts[k][first + i, 2 * block:3 * block, :] = exts[k][first + i, 0:block, :]
                    return carry
                lax.fori_loop(0, block, both, 0)

    def aperture(ext, i):
        parts = [ext[shift_x + i, pl.ds(shift_y + t, 8, turns), :] for t in range(turns)]
        return jnp.concatenate(parts, axis=0)

    def put_grad(grad, i, value):
        for t in range(turns):
            grad[i + block, pl.ds(block + t, 8, turns), :] = value[8 * t:8 * t + 8]

    def stage_b(rows):
        vz = []
        for i in rows:
            rho = aperture(ext_r, i)
            r = 1.0 / rho
            dens[i] = rho
            inv[i] = r
            t = -time_ratio * r
            vx1[i + 4] = t * ex[i]
            vy1[i] = t * ey[i]
            z = t * ez[i]
            vz1[i] = z
            vz.append(z)
        for i, d in zip(rows, along_z(vz, w_minus[...])):
            zd[i] = d

    def stage_c(rows):
        for i in rows:
            v = aperture(ext_v, i)
            k = time_ratio * dens[i] * v * v
            speed[i] = v
            s = dxy_minus(vx1, vy1, i) + zd[i]
            kk[i] = k
            s1[i] = s
            p1[i + 4] = p0[i + 4] - k * s

    def stage_d(rows):
        vz = []
        z = along_z([p1[i + 4] for i in rows], w_plus[...])
        for i, dz in zip(rows, z):
            t = -time_ratio * inv[i]
            vx2[i + 4] = vx1[i + 4] + t * dx_plus(p1, i)
            vy2[i] = vy1[i] + t * dy_plus(p1, i)
            v = vz1[i] + t * dz
            vz2[i] = v
            vz.append(v)
        for i, d in zip(rows, along_z(vz, w_minus[...])):
            zd[i] = d

    def stage_e(rows):
        for i in rows:
            s = dxy_minus(vx2, vy2, i) + zd[i]
            k = kk[i]
            q = p1[i + 4] - k * s - obs[i]
            q2[i] = q
            ss[i] = s * q
            a2[i + 4] = -k * q

    def stage_f(rows):
        bz = []
        z = along_z([a2[i + 4] for i in rows], w_plus[...])
        for i, dz in zip(rows, z):
            r = inv[i]
            dx = dx_plus(a2, i)
            dy = dy_plus(a2, i)
            rr[i] = dx * vx2[i + 4] + dy * vy2[i] + dz * vz2[i]
            bx[i + 4] = r * dx
            by[i] = r * dy
            bz.append(r * dz)
        for i, d in zip(rows, along_z(bz, w_minus[...])):
            zd[i] = d

    def stage_g(rows):
        for i in rows:
            q1 = q2[i] - time_ratio * (dxy_minus(bx, by, i) + zd[i])
            a1[i + 4] = -kk[i] * q1
            s = ss[i] + s1[i] * q1
            ss[i] = s
            put_grad(grad_v, i, -2.0 * time_ratio * dens[i] * speed[i] * s)

    def stage_h(rows):
        z = along_z([a1[i + 4] for i in rows], w_plus[...])
        for i, dz in zip(rows, z):
            total = rr[i] + dx_plus(a1, i) * vx1[i + 4]
            total = total + dy_plus(a1, i) * vy1[i] + dz * vz1[i]
            v = speed[i]
            put_grad(grad_r, i, inv[i] * total - time_ratio * v * v * ss[i])

    def back_line(k, h, piece, side):
        return remote(
            sl.at[k, piece, side, part(h)], rl.at[k, piece, side, part(h)],
            rl_s.at[k, h, piece, side], rl_r.at[k, h, piece, side], (to_side(side)[0], b),
        )

    def back_z(k, h):
        return remote(zs.at[k, part(h)], zr.at[k, part(h)], rz_s.at[k, h], rz_r.at[k, h], (a, behind))

    def back_y(k, h):
        return remote(ys.at[k, part(h)], yr.at[k, part(h)], ry_s.at[k, h], ry_r.at[k, h], (a, partner))

    def term(k, slot_x, slot_y, i):
        return grads[k][block + slot_x * block - shift_x + i, pl.ds(block + slot_y * block - shift_y, block), :]

    def send_line(k, piece):
        for h in range(PARTS):
            for side in sides:
                @pl.when(to_side(side)[1])
                def _():
                    def fill(i, carry):
                        if piece == 0:
                            sl[k, 0, side, i] = term(k, 2 * side, 1, i)
                        else:
                            sl[k, 1, side, i] = term(k, 2 * side, 0, i) + term(k, 2 * side, 2, i)
                        return carry
                    lax.fori_loop(h * rows_of, (h + 1) * rows_of, fill, 0)
                    back_line(k, h, piece, side).start()

    for side in range(2):
        @pl.when(jnp.logical_not(has_line[side]))
        def _():
            for k in range(2):
                for piece in range(2):
                    rl[k, piece, 1 - side] = jnp.zeros((block, block, depth), jnp.float32)

    @pl.when(jnp.logical_not(has_onward))
    def _():
        for k in range(2):
            zr[k] = jnp.zeros((block, block, depth), jnp.float32)

    finish_halo(1)
    over(stage_b, RB_Z)
    finish_halo(0)
    over(stage_c)
    over(stage_d, RB_Z)
    over(stage_e)
    over(stage_f, RB_Z)
    over(stage_g)
    send_line(0, 1)
    over(stage_h, RB_Z)
    send_line(1, 1)
    send_line(0, 0)
    send_line(1, 0)

    def wait_line(k, h, piece):
        for side in range(2):
            pl.when(has_line[side])(lambda: back_line(k, h, piece, 1 - side).wait_recv())

    def gather(k, h, slot, out, extra):
        def add(i, carry):
            for c in range(0, block, 8):
                cells = pl.ds(c, 8)
                total = grads[k][
                    2 * block - shift_x + i, pl.ds(block + slot * block - shift_y + c, 8), :
                ]
                for side in range(2):
                    if isinstance(slot, int):
                        total = total + rl[k, 0, 1 - side, i, cells, :]
                    else:
                        inside = (column + c - places[side]) * (1 - slot) - slot // 2 >= 0
                        total = total + jnp.where(inside, rl[k, 1, 1 - side, i, cells, :], 0.0)
                if extra is not None:
                    total = total + extra[k, i, cells, :]
                out[k, i, cells, :] = total
            return carry
        lax.fori_loop(h * rows_of, (h + 1) * rows_of, add, 0)

    for k, h in back_chunks:
        wait_line(k, h, 1)
        @pl.when(has_behind)
        def _():
            gather(k, h, far, zs, None)
            back_z(k, h).start()
    for k, h in back_chunks:
        pl.when(has_onward)(lambda: back_z(k, h).wait_recv())
        gather(k, h, near, ys, zr)
        back_y(k, h).start()
    for k, h in back_chunks:
        wait_line(k, h, 0)
        back_y(k, h).wait_recv()
        gather(k, h, 1, out, yr)

    for k, h in chunks:
        fwd_y(k, h).wait_send()
        back_y(k, h).wait_send()
        pl.when(has_onward)(lambda: fwd_z(k, h).wait_send())
        pl.when(has_behind)(lambda: back_z(k, h).wait_send())
        for side in range(2):
            @pl.when(has_line[side])
            def _():
                for piece in range(2):
                    fwd_line(k, h, piece, side).wait_send()
                    back_line(k, h, piece, side).wait_send()
    for side in range(2):
        pl.when(has_line[side])(lambda: tell(side).wait_send())


def apart(both, vel_out, rho_out):
    vel_out[...] = both[0]
    rho_out[...] = both[1]


def body(n_line, n_shot, velocity, density, start_pressure, observed, corners):
    block, _, depth = velocity.shape
    width = start_pressure.shape[0]
    cells = jax.ShapeDtypeStruct(velocity.shape, jnp.float32)

    def scratch(*shape):
        return pltpu.VMEM(shape, jnp.float32)

    along_x = scratch(width + 8, width, depth)
    plain = scratch(width, width, depth)
    extended = scratch(3 * block, 3 * block, depth)
    wide = scratch(2 * block + width, 2 * block + width, depth)
    matrix = pltpu.VMEM((2 * depth, 2 * depth), jnp.bfloat16)
    pieces = scratch(2, 2, 2, block, block, depth)
    place = pltpu.VMEM((8, depth), jnp.int32)
    places = pltpu.VMEM((2, 8, depth), jnp.int32)
    pair = scratch(2, block, block, depth)
    sem = pltpu.SemaphoreType.DMA
    vmem = pl.BlockSpec(memory_space=pltpu.VMEM)
    both = pl.pallas_call(
        functools.partial(kernel, n_line, n_shot),
        out_shape=jax.ShapeDtypeStruct((2,) + velocity.shape, jnp.float32),
        in_specs=[pl.BlockSpec(memory_space=pltpu.SMEM)] + [vmem] * 4,
        out_specs=vmem,
        scratch_shapes=[extended] * 2 + [wide] * 2 + [along_x] * 7 + [plain] * 18
        + [matrix] * 2 + [scratch(2, 2, block, block, depth)] + [pieces] * 2 + [pair] * 4 + [place, places]
        + [sem((2, PARTS))] * 4 + [sem((2, PARTS, 2, 2))] * 4 + [sem((2, PARTS))] * 4 + [sem((2,))] * 2,
        compiler_params=pltpu.CompilerParams(
            collective_id=0, has_side_effects=True, vmem_limit_bytes=36 * 1024 * 1024
        ),
    )(corners.reshape(2), velocity, density, start_pressure, observed)
    return pl.pallas_call(
        apart, out_shape=(cells, cells), in_specs=[vmem], out_specs=(vmem, vmem)
    )(both)


def solution(mesh):
    placed = P("line", "shot", None)
    return jax.shard_map(
        functools.partial(body, mesh.shape["line"], mesh.shape["shot"]),
        mesh=mesh,
        in_specs=(placed,) * 5,
        out_specs=(placed, placed),
        check_vma=False,
    )
```

```python
import functools

import jax
import jax.numpy as jnp
import ml_dtypes
import numpy as np
from jax import lax
from jax.experimental import pallas as pl
from jax.experimental.pallas import tpu as pltpu
from jax.sharding import PartitionSpec as P

MESH = pl.DeviceIdType.MESH
coeffs = (1225.0 / 1024.0, -245.0 / 3072.0, 49.0 / 5120.0, -5.0 / 7168.0)
time_ratio = 0.1
wavelet = (20.0, -12.0)
PARTS = 2
RB = 4
RB_Z = 16


def split(value):
    high = float(np.float32(value).astype(ml_dtypes.bfloat16))
    low = float(np.float32(value - high).astype(ml_dtypes.bfloat16))
    return high, low


def band(depth, plus):
    row = lax.broadcasted_iota(jnp.int32, (depth, depth), 0)
    col = lax.broadcasted_iota(jnp.int32, (depth, depth), 1)
    gap = row - col
    high = jnp.zeros((depth, depth), jnp.float32)
    low = jnp.zeros((depth, depth), jnp.float32)
    for m in range(1, 5):
        hi, lo = split(coeffs[m - 1])
        up, down = (m, 1 - m) if plus else (m - 1, -m)
        high = jnp.where(gap == up, hi, jnp.where(gap == down, -hi, high))
        low = jnp.where(gap == up, lo, jnp.where(gap == down, -lo, low))
    top = jnp.concatenate([high, low], axis=1)
    bottom = jnp.concatenate([high, jnp.zeros_like(low)], axis=1)
    return jnp.concatenate([top, bottom], axis=0).astype(jnp.bfloat16)


def along_z(rows, matrix):
    depth = rows[0].shape[1]
    width = rows[0].shape[0]
    field = jnp.concatenate(rows, axis=0)
    high = field.astype(jnp.bfloat16)
    low = (field - high.astype(jnp.float32)).astype(jnp.bfloat16)
    both = jnp.concatenate([high, low], axis=1)
    out = jnp.dot(both, matrix, preferred_element_type=jnp.float32)
    out = out[:, :depth] + out[:, depth:]
    return [out[k * width:(k + 1) * width] for k in range(len(rows))]


def combine(pairs):
    total = None
    for c, (upper, lower) in zip(coeffs, pairs):
        term = c * (upper - lower)
        total = term if total is None else total + term
    return total


def kernel(
    n_line, n_shot,
    corner, vel_in, rho_in, p_in, obs_in,
    out,
    ext_v, ext_r, grad_v, grad_r,
    p0, p1, a2, a1, vx1, vx2, bx, vy1, vy2, by,
    ex, ey, ez, zd, inv, kk, s1, ss, q2, vz1, vz2, rr, obs, dens, speed, w_plus, w_minus,
    p_here, obs_here, cs, sl, rl, zs, zr, ys, yr, place, places,
    fy_s, fy_r, fz_s, fz_r, fl_s, fl_r, rl_s, rl_r, rz_s, rz_r, ry_s, ry_r, at_s, at_r, in_s,
):
    block, _, depth = vel_in.shape
    width = p_in.shape[0]
    a = lax.axis_index("line")
    b = lax.axis_index("shot")
    odd = lax.rem(b, 2)
    partner = b + 1 - 2 * odd
    onward = b + 2 - 4 * odd
    behind = b - 2 + 4 * odd
    has_onward = (onward >= 0) & (onward < n_shot)
    has_behind = (behind >= 0) & (behind < n_shot)
    has_line = (a > 0, a < n_line - 1)
    rows_of = block // PARTS
    chunks = [(k, h) for k in (1, 0) for h in range(PARTS)]
    back_chunks = [(k, h) for k in (0, 1) for h in range(PARTS)]
    sides = (lax.rem(a, 2), 1 - lax.rem(a, 2))
    near = 2 * (1 - odd)
    far = 2 * odd
    exts = (ext_v, ext_r)
    ins = (vel_in, rho_in)
    grads = (grad_v, grad_r)

    barrier = pltpu.get_barrier_semaphore()

    def greet(there):
        pl.semaphore_signal(barrier, inc=1, device_id=there, device_id_type=MESH)

    greet((a, partner))
    pl.when(has_onward)(lambda: greet((a, onward)))
    pl.when(has_behind)(lambda: greet((a, behind)))
    pl.when(has_line[0])(lambda: greet((a - 1, b)))
    pl.when(has_line[1])(lambda: greet((a + 1, b)))
    mid = pl.ds(block, block)
    loads = [
        pltpu.make_async_copy(rho_in, ext_r.at[mid, mid, :], in_s.at[0]),
        pltpu.make_async_copy(vel_in, ext_v.at[mid, mid, :], in_s.at[1]),
        pltpu.make_async_copy(p_in, p_here, in_s.at[2]),
        pltpu.make_async_copy(obs_in, obs_here, in_s.at[3]),
    ]
    for load in loads:
        load.start()
    one = jnp.int32(1)
    none = jnp.int32(0)
    count = one
    for there in (has_onward, has_behind, has_line[0], has_line[1]):
        count = count + jnp.where(there, one, none)
    pl.semaphore_wait(barrier, count)

    def cols(slot):
        return pl.ds(pl.multiple_of(slot * block, block), block)

    def to_side(side):
        there = a - 1 + 2 * side
        return there, (there >= 0) & (there < n_line)

    def part(h, base=0):
        return pl.ds(base + h * rows_of, rows_of)

    def remote(src, dst, send, recv, there):
        return pltpu.make_async_remote_copy(
            src_ref=src, dst_ref=dst, send_sem=send, recv_sem=recv,
            device_id=there, device_id_type=MESH,
        )

    def fwd_y(k, h):
        return remote(
            ins[k].at[part(h)], exts[k].at[part(h, block), cols(far), :],
            fy_s.at[k, h], fy_r.at[k, h], (a, partner),
        )

    def fwd_z(k, h):
        return remote(
            exts[k].at[part(h, block), cols(near), :], exts[k].at[part(h, block), cols(far), :],
            fz_s.at[k, h], fz_r.at[k, h], (a, onward),
        )

    def fwd_line(k, h, piece, side):
        src = ins[k].at[part(h)] if piece == 0 else cs.at[k, side, part(h)]
        dst = exts[k].at[part(h, 2 * block * (1 - side)), cols(1 - piece), :]
        return remote(
            src, dst, fl_s.at[k, h, piece, side], fl_r.at[k, h, piece, side], (to_side(side)[0], b)
        )

    def start_line(k, h, piece):
        for side in sides:
            pl.when(to_side(side)[1])(lambda: fwd_line(k, h, piece, side).start())

    def tell(side):
        return remote(
            place, places.at[1 - side], at_s.at[side], at_r.at[1 - side], (to_side(side)[0], b)
        )

    shift_x = jnp.minimum(jnp.maximum(corner[0] - (a - 1) * block, 0), block)
    shift_y = jnp.minimum(jnp.maximum(corner[1] - (b - 1) * block, 0), block)
    place[...] = jnp.zeros((8, depth), jnp.int32) + shift_y
    for side in range(2):
        pl.when(has_line[side])(lambda: tell(side).start())

        @pl.when(jnp.logical_not(has_line[side]))
        def _():
            places[side] = jnp.zeros((8, depth), jnp.int32)

    for k, h in chunks:
        fwd_y(k, h).start()
        start_line(k, h, 0)

    for field in (p0, p1, a2, a1, vx1, vx2, bx):
        field[0:4, :, :] = jnp.zeros((4, width, depth), jnp.float32)
        field[width + 4:width + 8, :, :] = jnp.zeros((4, width, depth), jnp.float32)

    turns = width // 8

    def reorder(i, carry):
        for t in range(turns):
            p0[i + 4, 8 * t:8 * t + 8, :] = p_here[i, pl.ds(t, 8, turns), :]
            obs[i, 8 * t:8 * t + 8, :] = obs_here[i, pl.ds(t, 8, turns), :]
        return carry

    for load in loads:
        load.wait()
    lax.fori_loop(0, width, reorder, 0)
    w_plus[...] = band(depth, True)
    w_minus[...] = band(depth, False)
    wide = 2 * block + width

    def clear_grad(k):
        def clear(i, carry):
            grads[k][i] = jnp.zeros((wide, depth), jnp.float32)
            return carry
        lax.fori_loop(0, wide, clear, 0)

    def over(step, size=RB, first=0, last=width):
        def body(i, carry):
            step([i * size + k for k in range(size)])
            return carry
        lax.fori_loop(first // size, last // size, body, 0)

    sub = lax.broadcasted_iota(jnp.int32, (8, depth), 0)

    def reach(row):
        f = [row[8 * t:8 * t + 8] for t in range(turns)]
        down = [jnp.where(sub == 0, 0.0, pltpu.roll(x, 1, 0)) for x in f]
        up = [jnp.where(sub == 7, 0.0, pltpu.roll(x, 7, 0)) for x in f]
        return down + f + up

    def dx_plus(f, i):
        return combine([(f[i + 4 + m], f[i + 5 - m]) for m in range(1, 5)])

    def dy_plus(f, i):
        near_by = reach(f[i + 4])
        parts = []
        for t in range(turns, 2 * turns):
            parts.append(combine([(near_by[t + m], near_by[t + 1 - m]) for m in range(1, 5)]))
        return jnp.concatenate(parts, axis=0)

    def dxy_minus(fx, fy, i):
        near_by = reach(fy[i])
        total = None
        for m in range(1, 5):
            gap = fx[i + 3 + m] - fx[i + 4 - m]
            side = [near_by[t + m - 1] - near_by[t - m] for t in range(turns, 2 * turns)]
            term = coeffs[m - 1] * (gap + jnp.concatenate(side, axis=0))
            total = term if total is None else total + term
        return total

    def stage_a(rows):
        z = along_z([p0[i + 4] for i in rows], w_plus[...])
        for i, dz in zip(rows, z):
            ex[i] = dx_plus(p0, i)
            ey[i] = dy_plus(p0, i)
            ez[i] = dz

    def relay_near(k, h):
        fwd_y(k, h).wait_recv()
        pl.when(has_onward)(lambda: fwd_z(k, h).start())

    column = lax.broadcasted_iota(jnp.int32, (8, depth), 0)

    def relay_far(k, h):
        pl.when(has_behind)(lambda: fwd_z(k, h).wait_recv())
        for side in sides:
            @pl.when(to_side(side)[1])
            def _():
                start = places[side]
                def fill(i, carry):
                    for c in range(0, block, 8):
                        left = exts[k][block + i, c:c + 8, :]
                        right = exts[k][block + i, 2 * block + c:2 * block + c + 8, :]
                        cs[k, side, i, c:c + 8, :] = jnp.where(column + c >= start, left, right)
                    return carry
                lax.fori_loop(h * rows_of, (h + 1) * rows_of, fill, 0)
                fwd_line(k, h, 1, side).start()

    for side in range(2):
        pl.when(has_line[side])(lambda: tell(1 - side).wait_recv())

    for h in range(PARTS):
        relay_near(1, h)
        if h % (PARTS // 2) == 0:
            at = h // (PARTS // 2) * (width // 2)
            over(stage_a, RB_Z, at, at + width // 2)
    for h in range(PARTS):
        relay_near(0, h)
        relay_far(1, h)
        if h % (PARTS // 2) == 0:
            clear_grad(h // (PARTS // 2))
    for h in range(PARTS):
        relay_far(0, h)

    lane = lax.broadcasted_iota(jnp.int32, (1, depth), 1)
    spot = jnp.where(lane == depth // 2, 1.0, 0.0).astype(jnp.float32)
    half = width // 2
    at = 8 * (half % turns) + half // turns
    p0[half + 4, at:at + 1, :] = p0[half + 4, at:at + 1, :] + wavelet[0] * spot
    obs[half, at:at + 1, :] = obs[half, at:at + 1, :] - wavelet[1] * spot

    def finish_halo(k):
        for side in range(2):
            @pl.when(has_line[side])
            def _():
                for piece in range(2):
                    for h in range(PARTS):
                        fwd_line(k, h, piece, 1 - side).wait_recv()
                first = 2 * block * side
                def both(i, carry):
                    exts[k][first + i, 2 * block:3 * block, :] = exts[k][first + i, 0:block, :]
                    return carry
                lax.fori_loop(0, block, both, 0)

    def aperture(ext, i):
        parts = [ext[shift_x + i, pl.ds(shift_y + t, 8, turns), :] for t in range(turns)]
        return jnp.concatenate(parts, axis=0)

    def put_grad(grad, i, value):
        for t in range(turns):
            grad[i + block, pl.ds(block + t, 8, turns), :] = value[8 * t:8 * t + 8]

    def stage_b(rows):
        vz = []
        for i in rows:
            rho = aperture(ext_r, i)
            r = 1.0 / rho
            dens[i] = rho
            inv[i] = r
            t = -time_ratio * r
            vx1[i + 4] = t * ex[i]
            vy1[i] = t * ey[i]
            z = t * ez[i]
            vz1[i] = z
            vz.append(z)
        for i, d in zip(rows, along_z(vz, w_minus[...])):
            zd[i] = d

    def stage_c(rows):
        for i in rows:
            v = aperture(ext_v, i)
            k = time_ratio * dens[i] * v * v
            speed[i] = v
            s = dxy_minus(vx1, vy1, i) + zd[i]
            kk[i] = k
            s1[i] = s
            p1[i + 4] = p0[i + 4] - k * s

    def stage_d(rows):
        vz = []
        z = along_z([p1[i + 4] for i in rows], w_plus[...])
        for i, dz in zip(rows, z):
            t = -time_ratio * inv[i]
            vx2[i + 4] = vx1[i + 4] + t * dx_plus(p1, i)
            vy2[i] = vy1[i] + t * dy_plus(p1, i)
            v = vz1[i] + t * dz
            vz2[i] = v
            vz.append(v)
        for i, d in zip(rows, along_z(vz, w_minus[...])):
            zd[i] = d

    def stage_e(rows):
        for i in rows:
            s = dxy_minus(vx2, vy2, i) + zd[i]
            k = kk[i]
            q = p1[i + 4] - k * s - obs[i]
            q2[i] = q
            ss[i] = s * q
            a2[i + 4] = -k * q

    def stage_f(rows):
        bz = []
        z = along_z([a2[i + 4] for i in rows], w_plus[...])
        for i, dz in zip(rows, z):
            r = inv[i]
            dx = dx_plus(a2, i)
            dy = dy_plus(a2, i)
            rr[i] = dx * vx2[i + 4] + dy * vy2[i] + dz * vz2[i]
            bx[i + 4] = r * dx
            by[i] = r * dy
            bz.append(r * dz)
        for i, d in zip(rows, along_z(bz, w_minus[...])):
            zd[i] = d

    def stage_g(rows):
        for i in rows:
            q1 = q2[i] - time_ratio * (dxy_minus(bx, by, i) + zd[i])
            a1[i + 4] = -kk[i] * q1
            s = ss[i] + s1[i] * q1
            ss[i] = s
            put_grad(grad_v, i, -2.0 * time_ratio * dens[i] * speed[i] * s)

    def stage_h(rows):
        z = along_z([a1[i + 4] for i in rows], w_plus[...])
        for i, dz in zip(rows, z):
            total = rr[i] + dx_plus(a1, i) * vx1[i + 4]
            total = total + dy_plus(a1, i) * vy1[i] + dz * vz1[i]
            v = speed[i]
            put_grad(grad_r, i, inv[i] * total - time_ratio * v * v * ss[i])

    def back_line(k, h, piece, side):
        return remote(
            sl.at[k, piece, side, part(h)], rl.at[k, piece, side, part(h)],
            rl_s.at[k, h, piece, side], rl_r.at[k, h, piece, side], (to_side(side)[0], b),
        )

    def back_z(k, h):
        return remote(zs.at[k, part(h)], zr.at[k, part(h)], rz_s.at[k, h], rz_r.at[k, h], (a, behind))

    def back_y(k, h):
        return remote(ys.at[k, part(h)], yr.at[k, part(h)], ry_s.at[k, h], ry_r.at[k, h], (a, partner))

    def term(k, slot_x, slot_y, i):
        return grads[k][block + slot_x * block - shift_x + i, pl.ds(block + slot_y * block - shift_y, block), :]

    def send_line(k, piece):
        for h in range(PARTS):
            for side in sides:
                @pl.when(to_side(side)[1])
                def _():
                    def fill(i, carry):
                        if piece == 0:
                            sl[k, 0, side, i] = term(k, 2 * side, 1, i)
                        else:
                            sl[k, 1, side, i] = term(k, 2 * side, 0, i) + term(k, 2 * side, 2, i)
                        return carry
                    lax.fori_loop(h * rows_of, (h + 1) * rows_of, fill, 0)
                    back_line(k, h, piece, side).start()

    for side in range(2):
        @pl.when(jnp.logical_not(has_line[side]))
        def _():
            for k in range(2):
                for piece in range(2):
                    rl[k, piece, 1 - side] = jnp.zeros((block, block, depth), jnp.float32)

    @pl.when(jnp.logical_not(has_onward))
    def _():
        for k in range(2):
            zr[k] = jnp.zeros((block, block, depth), jnp.float32)

    finish_halo(1)
    over(stage_b, RB_Z)
    finish_halo(0)
    over(stage_c)
    over(stage_d, RB_Z)
    over(stage_e)
    over(stage_f, RB_Z)
    over(stage_g)
    send_line(0, 1)
    over(stage_h, RB_Z)
    send_line(1, 1)
    send_line(0, 0)
    send_line(1, 0)

    def wait_line(k, h, piece):
        for side in range(2):
            pl.when(has_line[side])(lambda: back_line(k, h, piece, 1 - side).wait_recv())

    def gather(k, h, slot, out, extra):
        def add(i, carry):
            for c in range(0, block, 8):
                cells = pl.ds(c, 8)
                total = grads[k][
                    2 * block - shift_x + i, pl.ds(block + slot * block - shift_y + c, 8), :
                ]
                for side in range(2):
                    if isinstance(slot, int):
                        total = total + rl[k, 0, 1 - side, i, cells, :]
                    else:
                        inside = (column + c - places[side]) * (1 - slot) - slot // 2 >= 0
                        total = total + jnp.where(inside, rl[k, 1, 1 - side, i, cells, :], 0.0)
                if extra is not None:
                    total = total + extra[k, i, cells, :]
                out[k, i, cells, :] = total
            return carry
        lax.fori_loop(h * rows_of, (h + 1) * rows_of, add, 0)

    for k, h in back_chunks:
        wait_line(k, h, 1)
        @pl.when(has_behind)
        def _():
            gather(k, h, far, zs, None)
            back_z(k, h).start()
    for k, h in back_chunks:
        pl.when(has_onward)(lambda: back_z(k, h).wait_recv())
        gather(k, h, near, ys, zr)
        back_y(k, h).start()
    for k, h in back_chunks:
        wait_line(k, h, 0)
        back_y(k, h).wait_recv()
        gather(k, h, 1, out, yr)

    for k, h in chunks:
        fwd_y(k, h).wait_send()
        back_y(k, h).wait_send()
        pl.when(has_onward)(lambda: fwd_z(k, h).wait_send())
        pl.when(has_behind)(lambda: back_z(k, h).wait_send())
        for side in range(2):
            @pl.when(has_line[side])
            def _():
                for piece in range(2):
                    fwd_line(k, h, piece, side).wait_send()
                    back_line(k, h, piece, side).wait_send()
    for side in range(2):
        pl.when(has_line[side])(lambda: tell(side).wait_send())


def apart(both, vel_out, rho_out):
    vel_out[...] = both[0]
    rho_out[...] = both[1]


def body(n_line, n_shot, velocity, density, start_pressure, observed, corners):
    block, _, depth = velocity.shape
    width = start_pressure.shape[0]
    cells = jax.ShapeDtypeStruct(velocity.shape, jnp.float32)

    def scratch(*shape):
        return pltpu.VMEM(shape, jnp.float32)

    along_x = scratch(width + 8, width, depth)
    plain = scratch(width, width, depth)
    extended = scratch(3 * block, 3 * block, depth)
    wide = scratch(2 * block + width, 2 * block + width, depth)
    matrix = pltpu.VMEM((2 * depth, 2 * depth), jnp.bfloat16)
    pieces = scratch(2, 2, 2, block, block, depth)
    place = pltpu.VMEM((8, depth), jnp.int32)
    places = pltpu.VMEM((2, 8, depth), jnp.int32)
    pair = scratch(2, block, block, depth)
    sem = pltpu.SemaphoreType.DMA
    vmem = pl.BlockSpec(memory_space=pltpu.VMEM)
    both = pl.pallas_call(
        functools.partial(kernel, n_line, n_shot),
        out_shape=jax.ShapeDtypeStruct((2,) + velocity.shape, jnp.float32),
        in_specs=[pl.BlockSpec(memory_space=pltpu.SMEM)] + [pl.BlockSpec(memory_space=pl.ANY)] * 4,
        out_specs=vmem,
        scratch_shapes=[extended] * 2 + [wide] * 2 + [along_x] * 7 + [plain] * 18
        + [matrix] * 2 + [plain] * 2 + [scratch(2, 2, block, block, depth)] + [pieces] * 2 + [pair] * 4 + [place, places]
        + [sem((2, PARTS))] * 4 + [sem((2, PARTS, 2, 2))] * 4 + [sem((2, PARTS))] * 4 + [sem((2,))] * 2 + [sem((4,))],
        compiler_params=pltpu.CompilerParams(
            collective_id=0, has_side_effects=True, vmem_limit_bytes=56 * 1024 * 1024
        ),
    )(corners.reshape(2), velocity, density, start_pressure, observed)
    return pl.pallas_call(
        apart, out_shape=(cells, cells), in_specs=[vmem], out_specs=(vmem, vmem)
    )(both)


def solution(mesh):
    placed = P("line", "shot", None)
    return jax.shard_map(
        functools.partial(body, mesh.shape["line"], mesh.shape["shot"]),
        mesh=mesh,
        in_specs=(placed,) * 5,
        out_specs=(placed, placed),
        check_vma=False,
    )
```

```python
import functools

import jax
import jax.numpy as jnp
import ml_dtypes
import numpy as np
from jax import lax
from jax.experimental import pallas as pl
from jax.experimental.pallas import tpu as pltpu
from jax.sharding import PartitionSpec as P

MESH = pl.DeviceIdType.MESH
coeffs = (1225.0 / 1024.0, -245.0 / 3072.0, 49.0 / 5120.0, -5.0 / 7168.0)
time_ratio = 0.1
wavelet = (20.0, -12.0)
PARTS = 4
RB = 4
RB_Z = 16


def split(value):
    high = float(np.float32(value).astype(ml_dtypes.bfloat16))
    low = float(np.float32(value - high).astype(ml_dtypes.bfloat16))
    return high, low


def band(depth, plus):
    row = lax.broadcasted_iota(jnp.int32, (depth, depth), 0)
    col = lax.broadcasted_iota(jnp.int32, (depth, depth), 1)
    gap = row - col
    high = jnp.zeros((depth, depth), jnp.float32)
    low = jnp.zeros((depth, depth), jnp.float32)
    for m in range(1, 5):
        hi, lo = split(coeffs[m - 1])
        up, down = (m, 1 - m) if plus else (m - 1, -m)
        high = jnp.where(gap == up, hi, jnp.where(gap == down, -hi, high))
        low = jnp.where(gap == up, lo, jnp.where(gap == down, -lo, low))
    top = jnp.concatenate([high, low], axis=1)
    bottom = jnp.concatenate([high, jnp.zeros_like(low)], axis=1)
    return jnp.concatenate([top, bottom], axis=0).astype(jnp.bfloat16)


def along_z(rows, matrix):
    depth = rows[0].shape[1]
    width = rows[0].shape[0]
    field = jnp.concatenate(rows, axis=0)
    high = field.astype(jnp.bfloat16)
    low = (field - high.astype(jnp.float32)).astype(jnp.bfloat16)
    both = jnp.concatenate([high, low], axis=1)
    out = jnp.dot(both, matrix, preferred_element_type=jnp.float32)
    out = out[:, :depth] + out[:, depth:]
    return [out[k * width:(k + 1) * width] for k in range(len(rows))]


def combine(pairs):
    total = None
    for c, (upper, lower) in zip(coeffs, pairs):
        term = c * (upper - lower)
        total = term if total is None else total + term
    return total


def kernel(
    n_line, n_shot,
    corner, vel_in, rho_in, p_in, obs_in,
    out,
    ext_v, ext_r, grad_v, grad_r,
    p0, p1, a2, a1, vx1, vx2, bx, vy1, vy2, by,
    ex, ey, ez, zd, inv, kk, s1, ss, q2, vz1, vz2, rr, obs, dens, speed, w_plus, w_minus,
    p_here, obs_here, cs, sl, rl, zs, zr, ys, yr, place, places,
    fy_s, fy_r, fz_s, fz_r, fl_s, fl_r, rl_s, rl_r, rz_s, rz_r, ry_s, ry_r, at_s, at_r, in_s,
):
    block, _, depth = vel_in.shape
    width = p_in.shape[0]
    a = lax.axis_index("line")
    b = lax.axis_index("shot")
    odd = lax.rem(b, 2)
    partner = b + 1 - 2 * odd
    onward = b + 2 - 4 * odd
    behind = b - 2 + 4 * odd
    has_onward = (onward >= 0) & (onward < n_shot)
    has_behind = (behind >= 0) & (behind < n_shot)
    has_line = (a > 0, a < n_line - 1)
    rows_of = block // PARTS
    chunks = [(k, h) for k in (1, 0) for h in range(PARTS)]
    back_chunks = [(k, h) for k in (0, 1) for h in range(PARTS)]
    sides = (lax.rem(a, 2), 1 - lax.rem(a, 2))
    near = 2 * (1 - odd)
    far = 2 * odd
    exts = (ext_v, ext_r)
    ins = (vel_in, rho_in)
    grads = (grad_v, grad_r)

    barrier = pltpu.get_barrier_semaphore()

    def greet(there):
        pl.semaphore_signal(barrier, inc=1, device_id=there, device_id_type=MESH)

    greet((a, partner))
    pl.when(has_onward)(lambda: greet((a, onward)))
    pl.when(has_behind)(lambda: greet((a, behind)))
    pl.when(has_line[0])(lambda: greet((a - 1, b)))
    pl.when(has_line[1])(lambda: greet((a + 1, b)))
    mid = pl.ds(block, block)
    loads = [
        pltpu.make_async_copy(rho_in, ext_r.at[mid, mid, :], in_s.at[0]),
        pltpu.make_async_copy(vel_in, ext_v.at[mid, mid, :], in_s.at[1]),
        pltpu.make_async_copy(p_in, p_here, in_s.at[2]),
        pltpu.make_async_copy(obs_in, obs_here, in_s.at[3]),
    ]
    for load in loads:
        load.start()
    one = jnp.int32(1)
    none = jnp.int32(0)
    count = one
    for there in (has_onward, has_behind, has_line[0], has_line[1]):
        count = count + jnp.where(there, one, none)
    pl.semaphore_wait(barrier, count)

    def cols(slot):
        return pl.ds(pl.multiple_of(slot * block, block), block)

    def to_side(side):
        there = a - 1 + 2 * side
        return there, (there >= 0) & (there < n_line)

    def part(h, base=0):
        return pl.ds(base + h * rows_of, rows_of)

    def remote(src, dst, send, recv, there):
        return pltpu.make_async_remote_copy(
            src_ref=src, dst_ref=dst, send_sem=send, recv_sem=recv,
            device_id=there, device_id_type=MESH,
        )

    def fwd_y(k, h):
        return remote(
            ins[k].at[part(h)], exts[k].at[part(h, block), cols(far), :],
            fy_s.at[k, h], fy_r.at[k, h], (a, partner),
        )

    def fwd_z(k, h):
        return remote(
            exts[k].at[part(h, block), cols(near), :], exts[k].at[part(h, block), cols(far), :],
            fz_s.at[k, h], fz_r.at[k, h], (a, onward),
        )

    def fwd_line(k, h, piece, side):
        src = ins[k].at[part(h)] if piece == 0 else cs.at[k, side, part(h)]
        dst = exts[k].at[part(h, 2 * block * (1 - side)), cols(1 - piece), :]
        return remote(
            src, dst, fl_s.at[k, h, piece, side], fl_r.at[k, h, piece, side], (to_side(side)[0], b)
        )

    def start_line(k, h, piece):
        for side in sides:
            pl.when(to_side(side)[1])(lambda: fwd_line(k, h, piece, side).start())

    def tell(side):
        return remote(
            place, places.at[1 - side], at_s.at[side], at_r.at[1 - side], (to_side(side)[0], b)
        )

    shift_x = jnp.minimum(jnp.maximum(corner[0] - (a - 1) * block, 0), block)
    shift_y = jnp.minimum(jnp.maximum(corner[1] - (b - 1) * block, 0), block)
    place[...] = jnp.zeros((8, depth), jnp.int32) + shift_y
    for side in range(2):
        pl.when(has_line[side])(lambda: tell(side).start())

        @pl.when(jnp.logical_not(has_line[side]))
        def _():
            places[side] = jnp.zeros((8, depth), jnp.int32)

    for k, h in chunks:
        fwd_y(k, h).start()
        start_line(k, h, 0)

    for field in (p0, p1, a2, a1, vx1, vx2, bx):
        field[0:4, :, :] = jnp.zeros((4, width, depth), jnp.float32)
        field[width + 4:width + 8, :, :] = jnp.zeros((4, width, depth), jnp.float32)

    turns = width // 8

    def reorder(i, carry):
        for t in range(turns):
            p0[i + 4, 8 * t:8 * t + 8, :] = p_here[i, pl.ds(t, 8, turns), :]
            obs[i, 8 * t:8 * t + 8, :] = obs_here[i, pl.ds(t, 8, turns), :]
        return carry

    for load in loads:
        load.wait()
    lax.fori_loop(0, width, reorder, 0)
    w_plus[...] = band(depth, True)
    w_minus[...] = band(depth, False)
    wide = 2 * block + width

    def clear_grad(k):
        def clear(i, carry):
            grads[k][i] = jnp.zeros((wide, depth), jnp.float32)
            return carry
        lax.fori_loop(0, wide, clear, 0)

    def over(step, size=RB, first=0, last=width):
        def body(i, carry):
            step([i * size + k for k in range(size)])
            return carry
        lax.fori_loop(first // size, last // size, body, 0)

    sub = lax.broadcasted_iota(jnp.int32, (8, depth), 0)

    def reach(row):
        f = [row[8 * t:8 * t + 8] for t in range(turns)]
        down = [jnp.where(sub == 0, 0.0, pltpu.roll(x, 1, 0)) for x in f]
        up = [jnp.where(sub == 7, 0.0, pltpu.roll(x, 7, 0)) for x in f]
        return down + f + up

    def dx_plus(f, i):
        return combine([(f[i + 4 + m], f[i + 5 - m]) for m in range(1, 5)])

    def dy_plus(f, i):
        near_by = reach(f[i + 4])
        parts = []
        for t in range(turns, 2 * turns):
            parts.append(combine([(near_by[t + m], near_by[t + 1 - m]) for m in range(1, 5)]))
        return jnp.concatenate(parts, axis=0)

    def dxy_minus(fx, fy, i):
        near_by = reach(fy[i])
        total = None
        for m in range(1, 5):
            gap = fx[i + 3 + m] - fx[i + 4 - m]
            side = [near_by[t + m - 1] - near_by[t - m] for t in range(turns, 2 * turns)]
            term = coeffs[m - 1] * (gap + jnp.concatenate(side, axis=0))
            total = term if total is None else total + term
        return total

    def stage_a(rows):
        z = along_z([p0[i + 4] for i in rows], w_plus[...])
        for i, dz in zip(rows, z):
            ex[i] = dx_plus(p0, i)
            ey[i] = dy_plus(p0, i)
            ez[i] = dz

    def relay_near(k, h):
        fwd_y(k, h).wait_recv()
        pl.when(has_onward)(lambda: fwd_z(k, h).start())

    column = lax.broadcasted_iota(jnp.int32, (8, depth), 0)

    def relay_far(k, h):
        pl.when(has_behind)(lambda: fwd_z(k, h).wait_recv())
        for side in sides:
            @pl.when(to_side(side)[1])
            def _():
                start = places[side]
                def fill(i, carry):
                    for c in range(0, block, 8):
                        left = exts[k][block + i, c:c + 8, :]
                        right = exts[k][block + i, 2 * block + c:2 * block + c + 8, :]
                        cs[k, side, i, c:c + 8, :] = jnp.where(column + c >= start, left, right)
                    return carry
                lax.fori_loop(h * rows_of, (h + 1) * rows_of, fill, 0)
                fwd_line(k, h, 1, side).start()

    for side in range(2):
        pl.when(has_line[side])(lambda: tell(1 - side).wait_recv())

    for h in range(PARTS):
        relay_near(1, h)
        if h % (PARTS // 2) == 0:
            at = h // (PARTS // 2) * (width // 2)
            over(stage_a, RB_Z, at, at + width // 2)
    for h in range(PARTS):
        relay_near(0, h)
        relay_far(1, h)
        if h % (PARTS // 2) == 0:
            clear_grad(h // (PARTS // 2))
    for h in range(PARTS):
        relay_far(0, h)

    lane = lax.broadcasted_iota(jnp.int32, (1, depth), 1)
    spot = jnp.where(lane == depth // 2, 1.0, 0.0).astype(jnp.float32)
    half = width // 2
    at = 8 * (half % turns) + half // turns
    p0[half + 4, at:at + 1, :] = p0[half + 4, at:at + 1, :] + wavelet[0] * spot
    obs[half, at:at + 1, :] = obs[half, at:at + 1, :] - wavelet[1] * spot

    def finish_halo(k):
        for side in range(2):
            @pl.when(has_line[side])
            def _():
                for piece in range(2):
                    for h in range(PARTS):
                        fwd_line(k, h, piece, 1 - side).wait_recv()
                first = 2 * block * side
                def both(i, carry):
                    exts[k][first + i, 2 * block:3 * block, :] = exts[k][first + i, 0:block, :]
                    return carry
                lax.fori_loop(0, block, both, 0)

    def aperture(ext, i):
        parts = [ext[shift_x + i, pl.ds(shift_y + t, 8, turns), :] for t in range(turns)]
        return jnp.concatenate(parts, axis=0)

    def put_grad(grad, i, value):
        for t in range(turns):
            grad[i + block, pl.ds(block + t, 8, turns), :] = value[8 * t:8 * t + 8]

    def stage_b(rows):
        vz = []
        for i in rows:
            rho = aperture(ext_r, i)
            r = 1.0 / rho
            dens[i] = rho
            inv[i] = r
            t = -time_ratio * r
            vx1[i + 4] = t * ex[i]
            vy1[i] = t * ey[i]
            z = t * ez[i]
            vz1[i] = z
            vz.append(z)
        for i, d in zip(rows, along_z(vz, w_minus[...])):
            zd[i] = d

    def stage_c(rows):
        for i in rows:
            v = aperture(ext_v, i)
            k = time_ratio * dens[i] * v * v
            speed[i] = v
            s = dxy_minus(vx1, vy1, i) + zd[i]
            kk[i] = k
            s1[i] = s
            p1[i + 4] = p0[i + 4] - k * s

    def stage_d(rows):
        vz = []
        z = along_z([p1[i + 4] for i in rows], w_plus[...])
        for i, dz in zip(rows, z):
            t = -time_ratio * inv[i]
            vx2[i + 4] = vx1[i + 4] + t * dx_plus(p1, i)
            vy2[i] = vy1[i] + t * dy_plus(p1, i)
            v = vz1[i] + t * dz
            vz2[i] = v
            vz.append(v)
        for i, d in zip(rows, along_z(vz, w_minus[...])):
            zd[i] = d

    def stage_e(rows):
        for i in rows:
            s = dxy_minus(vx2, vy2, i) + zd[i]
            k = kk[i]
            q = p1[i + 4] - k * s - obs[i]
            q2[i] = q
            ss[i] = s * q
            a2[i + 4] = -k * q

    def stage_f(rows):
        bz = []
        z = along_z([a2[i + 4] for i in rows], w_plus[...])
        for i, dz in zip(rows, z):
            r = inv[i]
            dx = dx_plus(a2, i)
            dy = dy_plus(a2, i)
            rr[i] = dx * vx2[i + 4] + dy * vy2[i] + dz * vz2[i]
            bx[i + 4] = r * dx
            by[i] = r * dy
            bz.append(r * dz)
        for i, d in zip(rows, along_z(bz, w_minus[...])):
            zd[i] = d

    def stage_g(rows):
        for i in rows:
            q1 = q2[i] - time_ratio * (dxy_minus(bx, by, i) + zd[i])
            a1[i + 4] = -kk[i] * q1
            s = ss[i] + s1[i] * q1
            ss[i] = s
            put_grad(grad_v, i, -2.0 * time_ratio * dens[i] * speed[i] * s)

    def stage_h(rows):
        z = along_z([a1[i + 4] for i in rows], w_plus[...])
        for i, dz in zip(rows, z):
            total = rr[i] + dx_plus(a1, i) * vx1[i + 4]
            total = total + dy_plus(a1, i) * vy1[i] + dz * vz1[i]
            v = speed[i]
            put_grad(grad_r, i, inv[i] * total - time_ratio * v * v * ss[i])

    def back_line(k, h, piece, side):
        return remote(
            sl.at[k, piece, side, part(h)], rl.at[k, piece, side, part(h)],
            rl_s.at[k, h, piece, side], rl_r.at[k, h, piece, side], (to_side(side)[0], b),
        )

    def back_z(k, h):
        return remote(zs.at[k, part(h)], zr.at[k, part(h)], rz_s.at[k, h], rz_r.at[k, h], (a, behind))

    def back_y(k, h):
        return remote(ys.at[k, part(h)], yr.at[k, part(h)], ry_s.at[k, h], ry_r.at[k, h], (a, partner))

    def term(k, slot_x, slot_y, i):
        return grads[k][block + slot_x * block - shift_x + i, pl.ds(block + slot_y * block - shift_y, block), :]

    def send_line(k, piece):
        for h in range(PARTS):
            for side in sides:
                @pl.when(to_side(side)[1])
                def _():
                    def fill(i, carry):
                        if piece == 0:
                            sl[k, 0, side, i] = term(k, 2 * side, 1, i)
                        else:
                            sl[k, 1, side, i] = term(k, 2 * side, 0, i) + term(k, 2 * side, 2, i)
                        return carry
                    lax.fori_loop(h * rows_of, (h + 1) * rows_of, fill, 0)
                    back_line(k, h, piece, side).start()

    for side in range(2):
        @pl.when(jnp.logical_not(has_line[side]))
        def _():
            for k in range(2):
                for piece in range(2):
                    rl[k, piece, 1 - side] = jnp.zeros((block, block, depth), jnp.float32)

    @pl.when(jnp.logical_not(has_onward))
    def _():
        for k in range(2):
            zr[k] = jnp.zeros((block, block, depth), jnp.float32)

    finish_halo(1)
    over(stage_b, RB_Z)
    finish_halo(0)
    over(stage_c)
    over(stage_d, RB_Z)
    over(stage_e)
    over(stage_f, RB_Z)
    over(stage_g)
    send_line(0, 1)
    over(stage_h, RB_Z)
    send_line(1, 1)
    send_line(0, 0)
    send_line(1, 0)

    def wait_line(k, h, piece):
        for side in range(2):
            pl.when(has_line[side])(lambda: back_line(k, h, piece, 1 - side).wait_recv())

    def gather(k, h, slot, out, extra):
        def add(i, carry):
            for c in range(0, block, 8):
                cells = pl.ds(c, 8)
                total = grads[k][
                    2 * block - shift_x + i, pl.ds(block + slot * block - shift_y + c, 8), :
                ]
                for side in range(2):
                    if isinstance(slot, int):
                        total = total + rl[k, 0, 1 - side, i, cells, :]
                    else:
                        inside = (column + c - places[side]) * (1 - slot) - slot // 2 >= 0
                        total = total + jnp.where(inside, rl[k, 1, 1 - side, i, cells, :], 0.0)
                if extra is not None:
                    total = total + extra[k, i, cells, :]
                out[k, i, cells, :] = total
            return carry
        lax.fori_loop(h * rows_of, (h + 1) * rows_of, add, 0)

    for k, h in back_chunks:
        wait_line(k, h, 1)
        @pl.when(has_behind)
        def _():
            gather(k, h, far, zs, None)
            back_z(k, h).start()
    for k, h in back_chunks:
        pl.when(has_onward)(lambda: back_z(k, h).wait_recv())
        gather(k, h, near, ys, zr)
        back_y(k, h).start()
    for k, h in back_chunks:
        wait_line(k, h, 0)
        back_y(k, h).wait_recv()
        gather(k, h, 1, out, yr)

    for k, h in chunks:
        fwd_y(k, h).wait_send()
        back_y(k, h).wait_send()
        pl.when(has_onward)(lambda: fwd_z(k, h).wait_send())
        pl.when(has_behind)(lambda: back_z(k, h).wait_send())
        for side in range(2):
            @pl.when(has_line[side])
            def _():
                for piece in range(2):
                    fwd_line(k, h, piece, side).wait_send()
                    back_line(k, h, piece, side).wait_send()
    for side in range(2):
        pl.when(has_line[side])(lambda: tell(side).wait_send())


def apart(both, vel_out, rho_out):
    vel_out[...] = both[0]
    rho_out[...] = both[1]


def body(n_line, n_shot, velocity, density, start_pressure, observed, corners):
    block, _, depth = velocity.shape
    width = start_pressure.shape[0]
    cells = jax.ShapeDtypeStruct(velocity.shape, jnp.float32)

    def scratch(*shape):
        return pltpu.VMEM(shape, jnp.float32)

    along_x = scratch(width + 8, width, depth)
    plain = scratch(width, width, depth)
    extended = scratch(3 * block, 3 * block, depth)
    wide = scratch(2 * block + width, 2 * block + width, depth)
    matrix = pltpu.VMEM((2 * depth, 2 * depth), jnp.bfloat16)
    pieces = scratch(2, 2, 2, block, block, depth)
    place = pltpu.VMEM((8, depth), jnp.int32)
    places = pltpu.VMEM((2, 8, depth), jnp.int32)
    pair = scratch(2, block, block, depth)
    sem = pltpu.SemaphoreType.DMA
    vmem = pl.BlockSpec(memory_space=pltpu.VMEM)
    both = pl.pallas_call(
        functools.partial(kernel, n_line, n_shot),
        out_shape=jax.ShapeDtypeStruct((2,) + velocity.shape, jnp.float32),
        in_specs=[pl.BlockSpec(memory_space=pltpu.SMEM)] + [pl.BlockSpec(memory_space=pl.ANY)] * 4,
        out_specs=vmem,
        scratch_shapes=[extended] * 2 + [wide] * 2 + [along_x] * 7 + [plain] * 18
        + [matrix] * 2 + [plain] * 2 + [scratch(2, 2, block, block, depth)] + [pieces] * 2 + [pair] * 4 + [place, places]
        + [sem((2, PARTS))] * 4 + [sem((2, PARTS, 2, 2))] * 4 + [sem((2, PARTS))] * 4 + [sem((2,))] * 2 + [sem((4,))],
        compiler_params=pltpu.CompilerParams(
            collective_id=0, has_side_effects=True, vmem_limit_bytes=56 * 1024 * 1024
        ),
    )(corners.reshape(2), velocity, density, start_pressure, observed)
    return pl.pallas_call(
        apart, out_shape=(cells, cells), in_specs=[vmem], out_specs=(vmem, vmem)
    )(both)


def solution(mesh):
    placed = P("line", "shot", None)
    return jax.shard_map(
        functools.partial(body, mesh.shape["line"], mesh.shape["shot"]),
        mesh=mesh,
        in_specs=(placed,) * 5,
        out_specs=(placed, placed),
        check_vma=False,
    )
```
